256 devices in a mesh: dp: 16 (over y_hi, x, core), tensor: 16 (over z, y_lo).
Axes of the slice: x: 4, y: 4 (y_hi: 2, y_lo: 2; y = y_hi * 2 + y_lo), z: 8, core: 2. Of those that a mesh axis runs over, the one named last changes fastest.
Arguments:
- tokens: bfloat16 [8192, 4096], P(('dp', 'tensor')), may hold values from -24 to 24
- grad_out: bfloat16 [8192, 4096], P(('dp', 'tensor')), may hold values from -24 to 24
- gate_weight: bfloat16 [4096, 8192], P('dp', 'tensor'), may hold values from -0.09375 to 0.09375
- up_weight: bfloat16 [4096, 8192], P('dp', 'tensor'), may hold values from -0.09375 to 0.09375
- down_weight: bfloat16 [8192, 4096], P('tensor', 'dp'), may hold values from -0.0625 to 0.0625
Outputs:
- grad_tokens: bfloat16 [8192, 4096], P(('dp', 'tensor'))
- grad_gate: bfloat16 [4096, 8192], P('dp', 'tensor')
- grad_up: bfloat16 [4096, 8192], P('dp', 'tensor')
- grad_down: bfloat16 [8192, 4096], P('tensor', 'dp')
The draws below stay inside these ranges and needn't reach their ends.
All inputs are finite; a program needn't handle non-finite values.
Results may differ from the reference program's by a relative error of at most 0.024.
Values may be sent and summed in bfloat16 or wider, within the bound.
A program may use at most 128 MiB of HBM per device.

```python
import jax
import jax.numpy as jnp
from jax import lax

D = 4096
FF = 8192
TOK_DEV = 32
TOKENS = 8192
N_DP = 16
N_TENSOR = 16


def spiked(values, key, source, target, blocks, factor):
    def block_of(dim):
        return (jnp.arange(values.shape[dim]) // (values.shape[dim] // blocks)).reshape((-1,) + (1,) * (values.ndim - 1 - dim))

    near = jax.random.permutation(key, blocks)[block_of(target)]
    other_side = (block_of(target) + blocks // 2) % blocks
    return jnp.where((block_of(source) == near) | (block_of(source) == other_side), factor * values, values)


def levels(key, extent, split, smallest, high):
    level = 1.0
    for axis_at, blocks in split:
        heights = jax.random.uniform(jax.random.fold_in(jax.random.fold_in(key, 6), axis_at), (blocks,), jnp.float32, smallest / len(split), high / len(split))
        level = level * jnp.repeat(jnp.exp(heights), extent[axis_at] // blocks).reshape((-1,) + (1,) * (len(extent) - 1 - axis_at))
    return level


def noise(own_key, extent, spread, reach, pieces=(), held_as=jnp.bfloat16):
    loudness = levels(own_key, extent, pieces, -0.22, 0.18) if pieces else 1.0
    entries = jax.random.normal(own_key, extent, jnp.float32) * spread * loudness
    return jnp.minimum(jnp.maximum(entries, -reach), reach).astype(held_as)


def bell_draw_with(stream_key, extent, deviation, most, cuts, heavy, kind=jnp.bfloat16):
    array = deviation * jax.random.normal(stream_key, extent, jnp.float32)
    if cuts:
        array = array * levels(stream_key, extent, cuts, -0.22, 0.18)
    return jnp.clip(spiked(array, jax.random.fold_in(stream_key, 3), *heavy), -most, most).astype(kind)


def setup_inputs(seed: int = 0) -> dict:
    key_list = jax.random.split(jax.random.key(seed), 6)
    tokens = bell_draw_with(key_list[0], (TOKENS, D), 1.0, 24.0, ((0, 256),), (0, 1, 256, 6.0))
    grad_out = bell_draw_with(key_list[1], (TOKENS, D), 1.0, 24.0, ((0, 256),), (0, 1, 256, 6.0))
    gate_weight = noise(key_list[2], (D, FF), D ** -0.5, 0.09375, ((0, 16), (1, 16)))
    up_weight = noise(key_list[3], (D, FF), D ** -0.5, 0.09375, ((0, 16), (1, 16)))
    down_weight = noise(key_list[4], (FF, D), FF ** -0.5, 0.0625, ((0, 16), (1, 16)))
    return {"tokens": tokens, "grad_out": grad_out, "gate_weight": gate_weight, "up_weight": up_weight, "down_weight": down_weight}


def round_partial(value):
    return lax.optimization_barrier(value.astype(jnp.bfloat16)).astype(jnp.float32)


def reference(tokens, grad_out, gate_weight, up_weight, down_weight):
    gate_value = jnp.dot(tokens, gate_weight, preferred_element_type=jnp.float32)
    up_value = jnp.dot(tokens, up_weight, preferred_element_type=jnp.float32)
    sigmoid_gate = jax.nn.sigmoid(gate_value)
    activated = gate_value * sigmoid_gate
    hidden = (activated * up_value).astype(jnp.bfloat16)
    grad_hidden = jnp.dot(grad_out, down_weight.T, preferred_element_type=jnp.float32)
    grad_upvalue = (grad_hidden * activated).astype(jnp.bfloat16)
    grad_gatevalue = (grad_hidden * up_value * sigmoid_gate * (1.0 + gate_value * (1.0 - sigmoid_gate))).astype(jnp.bfloat16)
    grad_tokens = (jnp.dot(grad_gatevalue, gate_weight.T, preferred_element_type=jnp.float32)
                   + jnp.dot(grad_upvalue, up_weight.T, preferred_element_type=jnp.float32)).astype(jnp.bfloat16)
    group_rows = TOK_DEV * N_TENSOR
    inputs = tokens.reshape(N_DP, group_rows, D)
    grads = grad_out.reshape(N_DP, group_rows, D)
    gates = grad_gatevalue.reshape(N_DP, group_rows, FF)
    ups = grad_upvalue.reshape(N_DP, group_rows, FF)
    hiddens = hidden.reshape(N_DP, group_rows, FF)

    def add_group(totals, items):
        group_in, group_grad, group_gate, group_up, group_hidden = items
        total_gate = totals[0] + round_partial(jnp.dot(group_in.T, group_gate, preferred_element_type=jnp.float32))
        total_up = totals[1] + round_partial(jnp.dot(group_in.T, group_up, preferred_element_type=jnp.float32))
        total_down = totals[2] + round_partial(jnp.dot(group_hidden.T, group_grad, preferred_element_type=jnp.float32))
        return (total_gate, total_up, total_down), None

    start_totals = (jnp.zeros((D, FF), jnp.float32), jnp.zeros((D, FF), jnp.float32), jnp.zeros((FF, D), jnp.float32))
    totals, _ = lax.scan(add_group, start_totals, (inputs, grads, gates, ups, hiddens))
    return (grad_tokens, totals[0].astype(jnp.bfloat16), totals[1].astype(jnp.bfloat16),
            totals[2].astype(jnp.bfloat16))
```

```python
import jax
import jax.numpy as jnp
from jax import lax
from jax.experimental import pallas as pl
from jax.experimental.pallas import tpu as pltpu
from jax.sharding import PartitionSpec as P

MESH = pl.DeviceIdType.MESH
BF, F32 = jnp.bfloat16, jnp.float32
NX, NZ = 4, 8
Q = 4


class Links:
    def __init__(self, send_sem, recv_sem):
        self.send_sem, self.recv_sem = send_sem, recv_sem
        self.index, self.sent = {}, []

    def at(self, name):
        return self.index.setdefault(name, len(self.index))

    def send(self, name, src, dst, device):
        i = self.at(name)
        copy = pltpu.make_async_remote_copy(
            src_ref=src, dst_ref=dst, send_sem=self.send_sem.at[i], recv_sem=self.recv_sem.at[i],
            device_id=device, device_id_type=MESH,
        )
        copy.start()
        self.sent.append(copy)

    def recv(self, name, ref, device):
        i = self.at(name)
        pltpu.make_async_remote_copy(
            src_ref=ref, dst_ref=ref, send_sem=self.send_sem.at[i], recv_sem=self.recv_sem.at[i],
            device_id=device, device_id_type=MESH,
        ).wait_recv()

    def finish(self):
        for copy in self.sent:
            copy.wait_send()


N_COPIES = 96


def dot(a, b, ca, cb):
    return lax.dot_general(a, b, (((ca,), (cb,)), ((), ())), preferred_element_type=F32)


def kernel(tok, grd, gw, uw, dw, o_tok, o_gate, o_up, o_down,
           tg, w, acc, gc, hid, px, sb, xh, xf, yr, gt, z1, zr, lr, send_sem, recv_sem, local_sem):
    rows, dm = tok.shape
    dd, ff = gw.shape
    half = dd // 2
    all_rows = 16 * rows
    qc = dm // Q
    dp, ten = lax.axis_index("dp"), lax.axis_index("tensor")
    yh, x, c = dp // 8, (dp // 2) % NX, dp % 2
    z, yl = ten // 2, ten % 2

    def dp_at(h, xx, cc):
        return h * 8 + (xx % NX) * 2 + cc

    def ten_at(zz, ll):
        return (zz % NZ) * 2 + ll

    oh, ol, oc = 1 - yh, 1 - yl, 1 - c
    sib = {"dp": dp_at(yh, x, oc)}
    far_y = {"dp": dp_at(oh, x, c)}
    x_to = ({"dp": dp_at(yh, x + 1, c)}, {"dp": dp_at(yh, x + NX - 1, c)})
    near_y = {"tensor": ten_at(z, ol)}
    z_to = ({"tensor": ten_at(z + 1, yl)}, {"tensor": ten_at(z + NZ - 1, yl)})
    peers = (sib, far_y, *x_to, near_y, *z_to)

    me_w, me_t = dp, ten
    locals_ = [
        pltpu.make_async_copy(src, dst, local_sem.at[i])
        for i, (src, dst) in enumerate((
            (tok, tg.at[me_t, 0]), (grd, tg.at[me_t, 1]),
            (gw, w.at[me_w, 0]), (uw, w.at[me_w, 1]), (dw, w.at[me_w, 2]),
        ))
    ]
    for copy in locals_:
        copy.start()
    barrier = pltpu.get_barrier_semaphore()
    for peer in peers:
        pl.semaphore_signal(barrier, inc=1, device_id=peer, device_id_type=MESH)
    pl.semaphore_wait(barrier, len(peers))
    for copy in locals_:
        copy.wait()

    net = Links(send_sem, recv_sem)

    def t_send(name, slot, device, part=None):
        ref = tg.at[slot] if part is None else tg.at[slot, part]
        net.send(name, ref, ref, device)

    def t_recv(name, slot, device, part=None):
        net.recv(name, tg.at[slot] if part is None else tg.at[slot, part], device)

    def w_ref(slot, part):
        return w.at[slot] if part is None else w.at[slot, :, pl.ds(part * half, half), :]

    def w_send(name, slot, device, part=None):
        net.send(name, w_ref(slot, part), w_ref(slot, part), device)

    def w_recv(name, slot, device, part=None):
        net.recv(name, w_ref(slot, part), device)

    sign = (1, -1)

    def x_slot(h, d, k):
        return dp_at(yh if h == 0 else oh, x + NX - sign[d] * k, c)

    def z_slot(l, d, k):
        return ten_at(z + NZ - sign[d] * k, yl if l == 0 else ol)

    def z_start(l):
        for d in range(2):
            t_send(("z", d, 0, l), z_slot(l, d, 0), z_to[d])

    def x_start(h):
        for d in range(2):
            w_send(("x", d, 0, h), x_slot(h, d, 0), x_to[d])

    def z_pass(l, k):
        for d in range(2):
            t_recv(("z", d, k - 1, l), z_slot(l, d, k), z_to[1 - d])
            t_send(("z", d, k, l), z_slot(l, d, k), z_to[d], d if k == 3 else None)

    def x_pass(h):
        for d in range(2):
            w_recv(("x", d, 0, h), x_slot(h, d, 1), x_to[1 - d])
            w_send(("x", d, 1, h), x_slot(h, d, 1), x_to[d], d)
            w_send(("sib", d, 1, h), x_slot(h, d, 1), sib)

    def x_end(h):
        for d in range(2):
            w_recv(("x", d, 1, h), x_slot(h, d, 2), x_to[1 - d], d)
            w_send(("sib", d, 2, h), x_slot(h, d, 2), sib, d)

    t_send("yl", me_t, near_y)
    z_start(0)
    x_start(0)
    w_send("yh", me_w, far_y)
    w_send(("sib", 0, 0, 0), me_w, sib)
    t_recv("yl", z_slot(1, 0, 0), near_y)
    z_start(1)
    z_pass(0, 1)
    x_pass(0)
    z_pass(1, 1)
    w_recv("yh", x_slot(1, 0, 0), far_y)
    x_start(1)
    w_send(("sib", 0, 0, 1), x_slot(1, 0, 0), sib)
    z_pass(0, 2)
    x_end(0)
    z_pass(1, 2)
    x_pass(1)
    z_pass(0, 3)
    x_end(1)
    z_pass(1, 3)

    def sib_slot(h, d, k):
        return dp_at(yh if h == 0 else oh, x + NX - sign[d] * k, oc)

    for h in range(2):
        w_recv(("sib", 0, 0, h), sib_slot(h, 0, 0), sib)
        for d in range(2):
            w_recv(("sib", d, 1, h), sib_slot(h, d, 1), sib)
            w_recv(("sib", d, 2, h), sib_slot(h, d, 2), sib, d)
    for l in range(2):
        for d in range(2):
            t_recv(("z", d, 3, l), z_slot(l, d, 4), z_to[1 - d], d)

    def columns(d):
        return pl.ds(pl.multiple_of(d * dd, dd), dd)

    def tok_cols(part, d):
        return tg[:, part, :, columns(d)].reshape(all_rows, dd)

    acc[...] = jnp.zeros_like(acc)

    @pl.loop(0, 16)
    def _(d):
        a = tok_cols(0, d)
        acc[0] += dot(a, w[d, 0], 1, 0)
        acc[1] += dot(a, w[d, 1], 1, 0)
        acc[2] += dot(tok_cols(1, d), w[d, 2], 1, 0)

    @pl.loop(0, all_rows // 64)
    def _(i):
        r = pl.ds(pl.multiple_of(i * 64, 64), 64)
        gate, up, grad_hidden = acc[0, r], acc[1, r], acc[2, r]
        sigmoid = 1.0 / (1.0 + jnp.exp(-gate))
        activated = gate * sigmoid
        hid[r] = (activated * up).astype(BF)
        gc[r, :ff] = (grad_hidden * up * sigmoid * (1.0 + gate * (1.0 - sigmoid))).astype(BF)
        gc[r, ff:] = (grad_hidden * activated).astype(BF)

    order = ((2, 1), (2, 0), (1, 1), (3, 1), (1, 0), (3, 0), (0, 1), (0, 0))

    def weight_part(o):
        steps, h = order[o]

        @pl.loop(0, 2)
        def _(k):
            d = dp_at(yh if h == 0 else oh, x + steps, lax.rem(c + k, 2))
            both = dot(tok_cols(0, d), gc[...], 0, 0)
            px[k, o, 0] = both[:, :ff].astype(BF)
            px[k, o, 1] = both[:, ff:].astype(BF)
            px[k, o, 2] = dot(tok_cols(1, d), hid[...], 0, 0).astype(BF)

        net.send(("core", o), px.at[1, o], sb.at[o], sib)

    def add(dst, *srcs):
        total = dst[...].astype(F32)
        for src in srcs:
            total += src[...].astype(F32)
        dst[...] = total.astype(BF)

    def core_sum(o):
        net.recv(("core", o), sb.at[o], sib)

        @pl.loop(0, 3)
        def _(j):
            add(px.at[0, o, j], sb.at[o, j])

    def halves(o, d):
        return px.at[0, o, :, pl.ds(d * half, half), :]

    def x_far(s):
        for d in range(2):
            net.send(("xh", d, s), halves(s, d), xh.at[d, s], x_to[d])

    def x_near(s):
        for d in range(2):
            o = 2 + 2 * s + d
            net.recv(("xh", d, s), xh.at[d, s], x_to[1 - d])

            @pl.loop(0, 3)
            def _(j):
                add(px.at[0, o, j, pl.ds(d * half, half), :], xh.at[d, s, j])

            net.send(("xf", d, s), px.at[0, o], xf.at[d, s], x_to[d])

    def x_last(s):
        for d in range(2):
            net.recv(("xf", d, s), xf.at[d, s], x_to[1 - d])

    def token_part(q):
        @pl.loop(0, dm // dd // Q)
        def _(i):
            d = q * (dm // dd // Q) + i
            part = dot(gc[:, :ff], w[d, 0], 1, 1) + dot(gc[:, ff:], w[d, 1], 1, 1)
            gt[q, :, :, columns(i)] = part.reshape(16, rows, dd).astype(BF)

    def gt_ref(q, steps):
        return gt.at[q, pl.ds(ten_at(z + NZ + steps, 0), 2)]

    def z_far(d, i):
        net.send(("z1", d, i), gt_ref(2 * d + i, 4), z1.at[d, i], z_to[d])

    def z_near(k):
        for i in range(Q):
            for d in range(2):
                q = (2 + i) % Q if d == 0 else i
                ref = gt_ref(q, sign[d] * (3 - k))
                if k == 0:
                    if q // 2 == d:
                        net.recv(("z1", d, q % 2), z1.at[d, q % 2], z_to[1 - d])
                        add(ref, z1.at[d, q % 2])
                else:
                    net.recv(("zr", d, k - 1, q), zr.at[d, k - 1, q], z_to[1 - d])
                    add(ref, zr.at[d, k - 1, q])
                net.send(("zr", d, k, q), ref, zr.at[d, k, q], z_to[d])

    weight_part(0)
    weight_part(1)
    core_sum(0)
    x_far(0)
    token_part(0)
    z_far(0, 0)
    token_part(2)
    z_far(1, 0)
    core_sum(1)
    x_far(1)
    token_part(1)
    z_far(0, 1)
    token_part(3)
    z_far(1, 1)
    weight_part(2)
    weight_part(3)
    z_near(0)
    core_sum(2)
    core_sum(3)
    x_near(0)
    weight_part(4)
    weight_part(5)
    core_sum(4)
    core_sum(5)
    x_near(1)
    z_near(1)
    weight_part(6)
    weight_part(7)
    core_sum(6)
    core_sum(7)
    z_near(2)
    x_last(0)

    @pl.loop(0, 3)
    def _(j):
        add(px.at[0, 6, j], xf.at[0, 0, j], xf.at[1, 0, j])

    net.send("yr", px.at[0, 6], yr, far_y)

    for i in range(Q):
        q = (2 + i) % Q
        for d in range(2):
            net.recv(("zr", d, 2, q), zr.at[d, 2, q], z_to[1 - d])
        to = gt.at[q, ten_at(z, ol)]
        add(to, zr.at[0, 2, q, ol], zr.at[1, 2, q, ol])
        net.send(("lr", q), to, lr.at[q], near_y)
    x_last(1)
    for i in range(Q):
        q = (2 + i) % Q
        net.recv(("lr", q), lr.at[q], near_y)
        o_tok[:, q * qc:(q + 1) * qc] = (
            gt[q, ten_at(z, yl)].astype(F32) + zr[0, 2, q, yl].astype(F32)
            + zr[1, 2, q, yl].astype(F32) + lr[q].astype(F32)
        ).astype(BF)
    net.recv("yr", yr, far_y)
    for j, out in enumerate((o_gate, o_up, o_down)):
        out[...] = (
            px[0, 7, j].astype(F32) + xf[0, 1, j].astype(F32)
            + xf[1, 1, j].astype(F32) + yr[j].astype(F32)
        ).astype(BF)
    net.finish()
    assert len(net.index) <= N_COPIES


def local(tokens, grad_out, gate_weight, up_weight, down_weight):
    rows, dm = tokens.shape
    dd, ff = gate_weight.shape
    qc = dm // Q
    shard = (3, dd, ff)
    any_space = pl.BlockSpec(memory_space=pl.ANY)
    in_vmem = pl.BlockSpec(memory_space=pltpu.VMEM)
    out = pl.pallas_call(
        kernel,
        out_shape=(
            jax.ShapeDtypeStruct((rows, dm), BF),
            jax.ShapeDtypeStruct((dd, ff), BF),
            jax.ShapeDtypeStruct((dd, ff), BF),
            jax.ShapeDtypeStruct((dd, ff), BF),
        ),
        in_specs=[any_space] * 5,
        out_specs=[in_vmem] * 4,
        scratch_shapes=[
            pltpu.VMEM((16, 2, rows, dm), BF),
            pltpu.VMEM((16, *shard), BF),
            pltpu.VMEM((3, 16 * rows, ff), F32),
            pltpu.VMEM((16 * rows, 2 * ff), BF),
            pltpu.VMEM((16 * rows, ff), BF),
            pltpu.VMEM((2, 8, *shard), BF),
            pltpu.VMEM((8, *shard), BF),
            pltpu.VMEM((2, 2, 3, dd // 2, ff), BF),
            pltpu.VMEM((2, 2, *shard), BF),
            pltpu.VMEM(shard, BF),
            pltpu.VMEM((Q, 16, rows, qc), BF),
            pltpu.VMEM((2, 2, 2, rows, qc), BF),
            pltpu.VMEM((2, 3, Q, 2, rows, qc), BF),
            pltpu.VMEM((Q, rows, qc), BF),
            pltpu.SemaphoreType.DMA((N_COPIES,)),
            pltpu.SemaphoreType.DMA((N_COPIES,)),
            pltpu.SemaphoreType.DMA((5,)),
        ],
        compiler_params=pltpu.CompilerParams(
            collective_id=0, has_side_effects=True, vmem_limit_bytes=63 * 1024 * 1024
        ),
    )(tokens, grad_out, gate_weight, up_weight, down_weight.T)
    return out[0], out[1], out[2], out[3].T


def solution(mesh):
    return jax.shard_map(
        local,
        mesh=mesh,
        in_specs=(
            P(("dp", "tensor"), None),
            P(("dp", "tensor"), None),
            P("dp", "tensor"),
            P("dp", "tensor"),
            P("tensor", "dp"),
        ),
        out_specs=(
            P(("dp", "tensor"), None),
            P("dp", "tensor"),
            P("dp", "tensor"),
            P("tensor", "dp"),
        ),
        check_vma=False,
    )
```

```python
import jax
import jax.numpy as jnp
from jax import lax
from jax.experimental import pallas as pl
from jax.experimental.pallas import tpu as pltpu
from jax.sharding import PartitionSpec as P

MESH = pl.DeviceIdType.MESH
BF, F32 = jnp.bfloat16, jnp.float32
NX, NZ = 4, 8
Q = 4


class Links:
    def __init__(self, send_sem, recv_sem):
        self.send_sem, self.recv_sem = send_sem, recv_sem
        self.index, self.sent = {}, []

    def at(self, name):
        return self.index.setdefault(name, len(self.index))

    def send(self, name, src, dst, device):
        i = self.at(name)
        copy = pltpu.make_async_remote_copy(
            src_ref=src, dst_ref=dst, send_sem=self.send_sem.at[i], recv_sem=self.recv_sem.at[i],
            device_id=device, device_id_type=MESH,
        )
        copy.start()
        self.sent.append(copy)

    def recv(self, name, ref, device):
        i = self.at(name)
        pltpu.make_async_remote_copy(
            src_ref=ref, dst_ref=ref, send_sem=self.send_sem.at[i], recv_sem=self.recv_sem.at[i],
            device_id=device, device_id_type=MESH,
        ).wait_recv()

    def finish(self):
        for copy in self.sent:
            copy.wait_send()


N_COPIES = 112


def dot(a, b, ca, cb):
    return lax.dot_general(a, b, (((ca,), (cb,)), ((), ())), preferred_element_type=F32)


ARRIVAL = ((0, 0), (0, 1), (0, 7), (0, 2), (0, 6), (0, 3), (0, 5), (0, 4),
           (1, 1), (1, 7), (1, 2), (1, 6), (1, 4), (1, 3), (1, 5), (1, 0))
PLACE = {shard: i for i, shard in enumerate(ARRIVAL)}
EARLY = 13
ORDER = ((2, 1), (2, 0), (1, 1), (3, 1), (1, 0), (3, 0), (0, 1), (0, 0))


def kernel(tok, grd, gw, uw, dw, o_tok, o_gate, o_up, o_down,
           tg, w, acc, gc, hid, px, sb, xh, xf, yr, bh, bf, by, gt, z1, zr, lr, dws,
           send_sem, recv_sem, local_sem):
    rows, dm = tok.shape
    dd, ff = gw.shape
    half = dd // 2
    qc = dm // Q
    dp, ten = lax.axis_index("dp"), lax.axis_index("tensor")
    yh, x, c = dp // 8, (dp // 2) % NX, dp % 2
    z, yl = ten // 2, ten % 2

    def dp_at(h, xx, cc):
        return h * 8 + (xx % NX) * 2 + cc

    def ten_at(zz, ll):
        return (zz % NZ) * 2 + ll

    oh, ol, oc = 1 - yh, 1 - yl, 1 - c
    sib = {"dp": dp_at(yh, x, oc)}
    far_y = {"dp": dp_at(oh, x, c)}
    x_to = ({"dp": dp_at(yh, x + 1, c)}, {"dp": dp_at(yh, x + NX - 1, c)})
    near_y = {"tensor": ten_at(z, ol)}
    z_to = ({"tensor": ten_at(z + 1, yl)}, {"tensor": ten_at(z + NZ - 1, yl)})
    peers = (sib, far_y, *x_to, near_y, *z_to)

    me_w = dp
    locals_ = [
        pltpu.make_async_copy(src, dst, local_sem.at[i])
        for i, (src, dst) in enumerate((
            (tok, tg.at[0, 0]), (grd, tg.at[0, 1]),
            (gw, w.at[me_w, 0]), (uw, w.at[me_w, 1]), (dw, dws),
        ))
    ]
    for copy in locals_:
        copy.start()
    barrier = pltpu.get_barrier_semaphore()
    for peer in peers:
        pl.semaphore_signal(barrier, inc=1, device_id=peer, device_id_type=MESH)
    for copy in locals_:
        copy.wait()
    w[me_w, 2] = dws[...].T
    pl.semaphore_wait(barrier, len(peers))

    net = Links(send_sem, recv_sem)
    sign = (1, -1)

    def t_ref(l, steps, part=None):
        place = PLACE[l, steps % NZ]
        return tg.at[place] if part is None else tg.at[place, part]

    def z_send(l, k):
        for d in range(2):
            part = d if k == 3 else None
            net.send(("z", d, k, l), t_ref(l, -sign[d] * k, part), t_ref(l, -sign[d] * (k + 1), part), z_to[d])

    def z_recv(l, k):
        for d in range(2):
            net.recv(("z", d, k - 1, l), t_ref(l, -sign[d] * k, d if k == 4 else None), z_to[1 - d])

    def l_send(*steps):
        for k in steps:
            net.send(("l", k), t_ref(0, k), t_ref(1, k), near_y)

    def l_recv(*steps):
        for k in steps:
            net.recv(("l", k), t_ref(1, k), near_y)

    def w_ref(slot, part):
        return w.at[slot] if part is None else w.at[slot, :, pl.ds(part * half, half), :]

    def w_send(name, slot, device, part=None):
        net.send(name, w_ref(slot, part), w_ref(slot, part), device)

    def w_recv(name, slot, device, part=None):
        net.recv(name, w_ref(slot, part), device)

    def x_slot(h, d, k, core):
        return dp_at(yh if h == 0 else oh, x + NX - sign[d] * k, core)

    def x_start(h):
        for d in range(2):
            w_send(("x", d, 0, h), x_slot(h, d, 0, c), x_to[d])

    def x_pass(h):
        for d in range(2):
            w_recv(("x", d, 0, h), x_slot(h, d, 1, c), x_to[1 - d])
            w_send(("x", d, 1, h), x_slot(h, d, 1, c), x_to[d], d)
            w_send(("sib", d, 1, h), x_slot(h, d, 1, c), sib)

    def x_end(h):
        for d in range(2):
            w_recv(("x", d, 1, h), x_slot(h, d, 2, c), x_to[1 - d], d)
            w_send(("sib", d, 2, h), x_slot(h, d, 2, c), sib, d)

    def ag_head():
        z_send(0, 0)
        x_start(0)
        w_send("yh", me_w, far_y)
        w_send(("sib", 0, 0, 0), me_w, sib)
        acc[...] = jnp.zeros_like(acc)

    def ag_tail():
        for h in range(2):
            w_recv(("sib", 0, 0, h), x_slot(h, 0, 0, oc), sib)
            for d in range(2):
                w_recv(("sib", d, 1, h), x_slot(h, d, 1, oc), sib)
                w_recv(("sib", d, 2, h), x_slot(h, d, 2, oc), sib, d)

    ag_head()
    z_recv(0, 1)
    z_send(0, 1)
    x_pass(0)
    w_recv("yh", x_slot(1, 0, 0, c), far_y)
    x_start(1)
    l_send(1, 7)
    w_send(("sib", 0, 0, 1), x_slot(1, 0, 0, c), sib)
    z_recv(0, 2)
    z_send(0, 2)
    z_recv(0, 3)
    z_send(0, 3)
    x_end(0)
    l_recv(1, 7)
    z_send(1, 1)
    z_recv(0, 4)
    l_send(4)
    x_pass(1)
    l_send(0)
    z_recv(1, 2)
    z_send(1, 2)
    x_end(1)
    ag_tail()
    l_recv(4)

    def columns(d):
        return pl.ds(pl.multiple_of(d * dd, dd), dd)

    def tok_cols(part, d, first=0, end=16):
        return tg[first:end, part, :, columns(d)].reshape((end - first) * rows, dd)

    def fwd(first, end):
        r = pl.ds(first * rows, (end - first) * rows)

        @pl.loop(0, 16)
        def _(d):
            a = tok_cols(0, d, first, end)
            acc[0, r] += dot(a, w[d, 0], 1, 0)
            acc[1, r] += dot(a, w[d, 1], 1, 0)
            acc[2, r] += dot(tok_cols(1, d, first, end), w[d, 2], 1, 0)

        @pl.loop(first, end)
        def _(i):
            r = pl.ds(pl.multiple_of(i * rows, rows), rows)
            gate, up, grad_hidden = acc[0, r], acc[1, r], acc[2, r]
            sigmoid = 1.0 / (1.0 + jnp.exp(-gate))
            activated = gate * sigmoid
            hid[r] = (activated * up).astype(BF)
            gc[r, :ff] = (grad_hidden * up * sigmoid * (1.0 + gate * (1.0 - sigmoid))).astype(BF)
            gc[r, ff:] = (grad_hidden * activated).astype(BF)

    fwd(0, EARLY)
    z_recv(1, 3)
    l_recv(0)
    fwd(EARLY, 16)

    def shard_of(o, k):
        steps, h = ORDER[o]
        return dp_at(yh if h == 0 else oh, x + steps, lax.rem(c + k, 2))

    def weight_a(o):
        @pl.loop(0, 2)
        def _(k):
            both = dot(tok_cols(0, shard_of(o, k)), gc[...], 0, 0)
            px[k, o, 0] = both[:, :ff].astype(BF)
            px[k, o, 1] = both[:, ff:].astype(BF)

        net.send(("ca", o), px.at[1, o, pl.ds(0, 2)], sb.at[o, pl.ds(0, 2)], sib)

    def weight_b(o):
        @pl.loop(0, 2)
        def _(k):
            px[k, o, 2] = dot(tok_cols(1, shard_of(o, k)), hid[...], 0, 0).astype(BF)

        net.send(("cb", o), px.at[1, o, 2], sb.at[o, 2], sib)

    def add(dst, *srcs):
        total = dst[...].astype(F32)
        for src in srcs:
            total += src[...].astype(F32)
        dst[...] = total.astype(BF)

    def core_a(o):
        net.recv(("ca", o), sb.at[o, pl.ds(0, 2)], sib)

        @pl.loop(0, 2)
        def _(j):
            add(px.at[0, o, j], sb.at[o, j])

    def core_b(o):
        net.recv(("cb", o), sb.at[o, 2], sib)
        add(px.at[0, o, 2], sb.at[o, 2])

    def far_a(s):
        for d in range(2):
            net.send(("xh", d, s), px.at[0, s, pl.ds(0, 2), pl.ds(d * half, half), :], xh.at[d, s], x_to[d])

    def near_a(s):
        for d in range(2):
            o = 2 + 2 * s + d
            net.recv(("xh", d, s), xh.at[d, s], x_to[1 - d])

            @pl.loop(0, 2)
            def _(j):
                add(px.at[0, o, j, pl.ds(d * half, half), :], xh.at[d, s, j])

            net.send(("xf", d, s), px.at[0, o, pl.ds(0, 2)], xf.at[d, s], x_to[d])

    def last_a(s):
        for d in range(2):
            net.recv(("xf", d, s), xf.at[d, s], x_to[1 - d])

    B_OTHER, B_OWN = (0, 2, 3, 6), (1, 4, 5, 7)

    def cross_b(i):
        net.send(("by", i), px.at[0, B_OTHER[i], 2], by.at[i], far_y)

    def crossed_b(i):
        net.recv(("by", i), by.at[i], far_y)
        add(px.at[0, B_OWN[i], 2], by.at[i])

    def far_b():
        for d in range(2):
            net.send(("bh", d), px.at[0, 1, 2, pl.ds(d * half, half), :], bh.at[d], x_to[d])

    def near_b():
        for d in range(2):
            o = B_OWN[1 + d]
            net.recv(("bh", d), bh.at[d], x_to[1 - d])
            add(px.at[0, o, 2, pl.ds(d * half, half), :], bh.at[d])
            net.send(("bf", d), px.at[0, o, 2], bf.at[d], x_to[d])

    def token_part(q):
        @pl.loop(0, dm // dd // Q)
        def _(i):
            d = q * (dm // dd // Q) + i
            part = dot(gc[:, :ff], w[d, 0], 1, 1) + dot(gc[:, ff:], w[d, 1], 1, 1)
            part = part.reshape(16, rows, dd).astype(BF)
            for n, (l, steps) in enumerate(ARRIVAL):
                gt[q, steps, l, :, columns(i)] = part[n]

    def gt_ref(q, steps):
        return gt.at[q, steps % NZ]

    def z_far(d, i):
        net.send(("z1", d, i), gt_ref(2 * d + i, 4), z1.at[d, i], z_to[d])

    def z_near(k, i):
        for d in range(2):
            q = (2 + i) % Q if d == 0 else i
            ref = gt_ref(q, sign[d] * (3 - k))
            if k > 0:
                net.recv(("zr", d, k - 1, q), zr.at[d, k - 1, q], z_to[1 - d])
                add(ref, zr.at[d, k - 1, q])
            elif q // 2 == d:
                net.recv(("z1", d, q % 2), z1.at[d, q % 2], z_to[1 - d])
                add(ref, z1.at[d, q % 2])
            net.send(("zr", d, k, q), ref, zr.at[d, k, q], z_to[d])

    def z_last(i):
        q = (2 + i) % Q
        for d in range(2):
            net.recv(("zr", d, 2, q), zr.at[d, 2, q], z_to[1 - d])
        add(gt.at[q, 0, 1], zr.at[0, 2, q, 1], zr.at[1, 2, q, 1])
        net.send(("lr", q), gt.at[q, 0, 1], lr.at[q], near_y)

    def l_last(i):
        q = (2 + i) % Q
        net.recv(("lr", q), lr.at[q], near_y)
        o_tok[:, q * qc:(q + 1) * qc] = (
            gt[q, 0, 0].astype(F32) + zr[0, 2, q, 0].astype(F32)
            + zr[1, 2, q, 0].astype(F32) + lr[q].astype(F32)
        ).astype(BF)

    def cross_a():
        last_a(0)

        @pl.loop(0, 2)
        def _(j):
            add(px.at[0, 6, j], xf.at[0, 0, j], xf.at[1, 0, j])

        net.send("yr", px.at[0, 6, pl.ds(0, 2)], yr, far_y)

    weight_a(0)
    token_part(0)
    z_far(0, 0)
    core_a(0)
    far_a(0)
    token_part(2)
    z_far(1, 0)
    weight_a(1)
    weight_b(0)
    token_part(1)
    z_far(0, 1)
    core_a(1)
    far_a(1)
    core_b(0)
    cross_b(0)
    token_part(3)
    z_far(1, 1)
    z_near(0, 0)
    z_near(0, 1)
    weight_a(2)
    weight_a(3)
    weight_b(2)
    weight_b(3)
    core_a(2)
    core_a(3)
    near_a(0)
    core_b(2)
    core_b(3)
    cross_b(1)
    cross_b(2)
    z_near(0, 2)
    z_near(0, 3)
    weight_b(1)
    weight_b(6)
    weight_a(4)
    core_b(1)
    crossed_b(0)
    far_b()
    core_b(6)
    cross_b(3)
    z_near(1, 0)
    weight_a(5)
    core_a(4)
    core_a(5)
    near_a(1)
    z_near(1, 1)
    weight_b(4)
    weight_b(5)
    z_near(1, 2)
    weight_a(6)
    z_near(1, 3)
    core_b(4)
    core_b(5)
    core_a(6)
    cross_a()
    z_near(2, 0)
    crossed_b(1)
    crossed_b(2)
    near_b()
    z_near(2, 1)
    weight_a(7)
    z_near(2, 2)
    weight_b(7)
    z_near(2, 3)
    core_a(7)
    core_b(7)
    crossed_b(3)
    z_last(0)
    z_last(1)
    last_a(1)
    z_last(2)
    z_last(3)
    for i in range(Q):
        l_last(i)
    net.recv("yr", yr, far_y)
    for j, out in enumerate((o_gate, o_up)):
        out[...] = (
            px[0, 7, j].astype(F32) + xf[0, 1, j].astype(F32)
            + xf[1, 1, j].astype(F32) + yr[j].astype(F32)
        ).astype(BF)
    for d in range(2):
        net.recv(("bf", d), bf.at[d], x_to[1 - d])
    o_down[...] = (
        px[0, 7, 2].astype(F32) + bf[0].astype(F32) + bf[1].astype(F32)
    ).T.astype(BF)
    net.finish()
    assert len(net.index) <= N_COPIES


def local(tokens, grad_out, gate_weight, up_weight, down_weight):
    rows, dm = tokens.shape
    dd, ff = gate_weight.shape
    qc = dm // Q
    any_space = pl.BlockSpec(memory_space=pl.ANY)
    in_vmem = pl.BlockSpec(memory_space=pltpu.VMEM)
    return pl.pallas_call(
        kernel,
        out_shape=(
            jax.ShapeDtypeStruct((rows, dm), BF),
            jax.ShapeDtypeStruct((dd, ff), BF),
            jax.ShapeDtypeStruct((dd, ff), BF),
            jax.ShapeDtypeStruct((ff, dd), BF),
        ),
        in_specs=[any_space] * 5,
        out_specs=[in_vmem] * 4,
        scratch_shapes=[
            pltpu.VMEM((16, 2, rows, dm), BF),
            pltpu.VMEM((16, 3, dd, ff), BF),
            pltpu.VMEM((3, 16 * rows, ff), F32),
            pltpu.VMEM((16 * rows, 2 * ff), BF),
            pltpu.VMEM((16 * rows, ff), BF),
            pltpu.VMEM((2, 8, 3, dd, ff), BF),
            pltpu.VMEM((8, 3, dd, ff), BF),
            pltpu.VMEM((2, 2, 2, dd // 2, ff), BF),
            pltpu.VMEM((2, 2, 2, dd, ff), BF),
            pltpu.VMEM((2, dd, ff), BF),
            pltpu.VMEM((2, dd // 2, ff), BF),
            pltpu.VMEM((2, dd, ff), BF),
            pltpu.VMEM((4, dd, ff), BF),
            pltpu.VMEM((Q, NZ, 2, rows, qc), BF),
            pltpu.VMEM((2, 2, 2, rows, qc), BF),
            pltpu.VMEM((2, 3, Q, 2, rows, qc), BF),
            pltpu.VMEM((Q, rows, qc), BF),
            pltpu.VMEM((ff, dd), BF),
            pltpu.SemaphoreType.DMA((N_COPIES,)),
            pltpu.SemaphoreType.DMA((N_COPIES,)),
            pltpu.SemaphoreType.DMA((5,)),
        ],
        compiler_params=pltpu.CompilerParams(
            collective_id=0, has_side_effects=True, vmem_limit_bytes=63 * 1024 * 1024
        ),
    )(tokens, grad_out, gate_weight, up_weight, down_weight)


def solution(mesh):
    return jax.shard_map(
        local,
        mesh=mesh,
        in_specs=(
            P(("dp", "tensor"), None),
            P(("dp", "tensor"), None),
            P("dp", "tensor"),
            P("dp", "tensor"),
            P("tensor", "dp"),
        ),
        out_specs=(
            P(("dp", "tensor"), None),
            P("dp", "tensor"),
            P("dp", "tensor"),
            P("tensor", "dp"),
        ),
        check_vma=False,
    )
```

```python
import jax
import jax.numpy as jnp
from jax import lax
from jax.experimental import pallas as pl
from jax.experimental.pallas import tpu as pltpu
from jax.sharding import PartitionSpec as P

MESH = pl.DeviceIdType.MESH
BF, F32 = jnp.bfloat16, jnp.float32
NX, NZ = 4, 8
Q = 4


class Links:
    def __init__(self, send_sem, recv_sem):
        self.send_sem, self.recv_sem = send_sem, recv_sem
        self.index, self.sent = {}, []

    def at(self, name):
        return self.index.setdefault(name, len(self.index))

    def send(self, name, src, dst, device):
        i = self.at(name)
        copy = pltpu.make_async_remote_copy(
            src_ref=src, dst_ref=dst, send_sem=self.send_sem.at[i], recv_sem=self.recv_sem.at[i],
            device_id=device, device_id_type=MESH,
        )
        copy.start()
        self.sent.append(copy)

    def recv(self, name, ref, device):
        i = self.at(name)
        pltpu.make_async_remote_copy(
            src_ref=ref, dst_ref=ref, send_sem=self.send_sem.at[i], recv_sem=self.recv_sem.at[i],
            device_id=device, device_id_type=MESH,
        ).wait_recv()

    def finish(self):
        for copy in self.sent:
            copy.wait_send()


N_COPIES = 144


def dot(a, b, ca, cb):
    return lax.dot_general(a, b, (((ca,), (cb,)), ((), ())), preferred_element_type=F32)


ARRIVAL = ((0, 0), (0, 1), (0, 7), (0, 2), (0, 6), (0, 3), (0, 5), (0, 4),
           (1, 1), (1, 7), (1, 2), (1, 6), (1, 4), (1, 3), (1, 5), (1, 0))
PLACE = {shard: i for i, shard in enumerate(ARRIVAL)}
EARLY = 10
ORDER = ((2, 1), (2, 0), (1, 1), (3, 1), (1, 0), (3, 0), (0, 1), (0, 0))


def kernel(tok, grd, gw, uw, dw, o_tok, o_gate, o_up, o_down,
           tg, w, acc, gc, hid, px, sb, xh, xf, yr, bh, bf, by, gt, z1, zr, lr, dws,
           send_sem, recv_sem, local_sem):
    rows, dm = tok.shape
    dd, ff = gw.shape
    half = dd // 2
    qc = dm // Q
    dp, ten = lax.axis_index("dp"), lax.axis_index("tensor")
    yh, x, c = dp // 8, (dp // 2) % NX, dp % 2
    z, yl = ten // 2, ten % 2

    def dp_at(h, xx, cc):
        return h * 8 + (xx % NX) * 2 + cc

    def ten_at(zz, ll):
        return (zz % NZ) * 2 + ll

    oh, ol, oc = 1 - yh, 1 - yl, 1 - c
    sib = {"dp": dp_at(yh, x, oc)}
    far_y = {"dp": dp_at(oh, x, c)}
    x_to = ({"dp": dp_at(yh, x + 1, c)}, {"dp": dp_at(yh, x + NX - 1, c)})
    near_y = {"tensor": ten_at(z, ol)}
    z_to = ({"tensor": ten_at(z + 1, yl)}, {"tensor": ten_at(z + NZ - 1, yl)})
    peers = (sib, far_y, *x_to, near_y, *z_to)

    me_w = dp
    locals_ = [
        pltpu.make_async_copy(src, dst, local_sem.at[i])
        for i, (src, dst) in enumerate((
            (tok, tg.at[0, 0]), (grd, tg.at[0, 1]),
            (gw, w.at[me_w, 0]), (uw, w.at[me_w, 1]), (dw, dws),
        ))
    ]
    for copy in locals_:
        copy.start()
    barrier = pltpu.get_barrier_semaphore()
    for peer in peers:
        pl.semaphore_signal(barrier, inc=1, device_id=peer, device_id_type=MESH)
    for copy in locals_:
        copy.wait()
    w[me_w, 2] = dws[...].T
    pl.semaphore_wait(barrier, len(peers))

    net = Links(send_sem, recv_sem)
    sign = (1, -1)

    def t_ref(l, steps, part=None):
        place = PLACE[l, steps % NZ]
        return tg.at[place] if part is None else tg.at[place, part]

    def z_send(l, k, part):
        for d in range(2):
            if k < 3 or part == d:
                net.send(("z", d, k, l, part), t_ref(l, -sign[d] * k, part), t_ref(l, -sign[d] * (k + 1), part), z_to[d])

    def z_recv(l, k, part):
        for d in range(2):
            if k < 4 or part == d:
                net.recv(("z", d, k - 1, l, part), t_ref(l, -sign[d] * k, part), z_to[1 - d])

    def z_pass(l, k):
        for part in range(2):
            z_recv(l, k, part)
            z_send(l, k, part)

    def l_send(part, *steps):
        for k in steps:
            net.send(("l", k, part), t_ref(0, k, part), t_ref(1, k, part), near_y)

    def l_recv(part, *steps):
        for k in steps:
            net.recv(("l", k, part), t_ref(1, k, part), near_y)

    def w_ref(slot, part):
        return w.at[slot] if part is None else w.at[slot, :, pl.ds(part * half, half), :]

    def w_send(name, slot, device, part=None):
        net.send(name, w_ref(slot, part), w_ref(slot, part), device)

    def w_recv(name, slot, device, part=None):
        net.recv(name, w_ref(slot, part), device)

    def x_slot(h, d, k, core):
        return dp_at(yh if h == 0 else oh, x + NX - sign[d] * k, core)

    def x_start(h):
        for d in range(2):
            w_send(("x", d, 0, h), x_slot(h, d, 0, c), x_to[d])

    def x_pass(h):
        for d in range(2):
            w_recv(("x", d, 0, h), x_slot(h, d, 1, c), x_to[1 - d])
            w_send(("x", d, 1, h), x_slot(h, d, 1, c), x_to[d], d)
            w_send(("sib", d, 1, h), x_slot(h, d, 1, c), sib)

    def x_end(h):
        for d in range(2):
            w_recv(("x", d, 1, h), x_slot(h, d, 2, c), x_to[1 - d], d)
            w_send(("sib", d, 2, h), x_slot(h, d, 2, c), sib, d)

    def ag_head():
        z_send(0, 0, 0)
        x_start(0)
        z_send(0, 0, 1)
        w_send("yh", me_w, far_y)
        w_send(("sib", 0, 0, 0), me_w, sib)
        acc[...] = jnp.zeros_like(acc)

    def sib_recv(h):
        w_recv(("sib", 0, 0, h), x_slot(h, 0, 0, oc), sib)
        for d in range(2):
            w_recv(("sib", d, 1, h), x_slot(h, d, 1, oc), sib)

    def sib_end(h):
        for d in range(2):
            w_recv(("sib", d, 2, h), x_slot(h, d, 2, oc), sib, d)

    def columns(d):
        return pl.ds(pl.multiple_of(d * dd, dd), dd)

    def tok_cols(part, d, first=0, end=16):
        return tg[first:end, part, :, columns(d)].reshape((end - first) * rows, dd)

    def fwd(first, end, begin, stop, parts):
        r = pl.ds(first * rows, (end - first) * rows)

        @pl.loop(begin, stop)
        def _(pair):
            d = dp_at((yh + pair // 4) % 2, x + pair % 4 + 3, 0)
            both = pl.ds(pl.multiple_of(d * dd, 2 * dd), 2 * dd)

            def product(part, weight):
                a = tg[first:end, part, :, both].reshape((end - first) * rows, 2 * dd)
                return dot(a, w[pl.ds(d, 2), weight].reshape(2 * dd, ff), 1, 0)

            if 0 in parts:
                acc[0, r] += product(0, 0)
                acc[1, r] += product(0, 1)
            if 1 in parts:
                acc[2, r] += product(1, 2)

    def elem(first, end):
        @pl.loop(first, end)
        def _(i):
            r = pl.ds(pl.multiple_of(i * rows, rows), rows)
            gate, up, grad_hidden = acc[0, r], acc[1, r], acc[2, r]
            sigmoid = 1.0 / (1.0 + jnp.exp(-gate))
            activated = gate * sigmoid
            hid[r] = (activated * up).astype(BF)
            gc[r, :ff] = (grad_hidden * up * sigmoid * (1.0 + gate * (1.0 - sigmoid))).astype(BF)
            gc[r, ff:] = (grad_hidden * activated).astype(BF)

    ag_head()
    z_pass(0, 1)
    x_pass(0)
    w_recv("yh", x_slot(1, 0, 0, c), far_y)
    x_start(1)
    l_send(0, 1, 7)
    l_send(1, 1, 7)
    w_send(("sib", 0, 0, 1), x_slot(1, 0, 0, c), sib)
    z_pass(0, 2)
    z_pass(0, 3)
    x_end(0)
    for part in range(2):
        l_recv(part, 1, 7)
        z_send(1, 1, part)
    for part in range(2):
        z_recv(0, 4, part)
        l_send(part, 4)
    x_pass(1)
    l_send(0, 0)
    l_send(1, 0)
    sib_recv(0)
    sib_end(0)
    sib_recv(1)
    fwd(0, EARLY, 0, 7, (0, 1))
    z_pass(1, 2)
    x_end(1)
    sib_end(1)
    fwd(0, EARLY, 7, 8, (0, 1))
    elem(0, EARLY)
    for part in range(2):
        l_recv(part, 4)
        z_recv(1, 3, part)
        l_recv(part, 0)
        fwd(EARLY, 16, 0, 8, (part,))
    elem(EARLY, 16)

    def shard_of(o, k):
        steps, h = ORDER[o]
        return dp_at(yh if h == 0 else oh, x + steps, lax.rem(c + k, 2))

    def weight_a(o):
        @pl.loop(0, 2)
        def _(k):
            both = dot(tok_cols(0, shard_of(o, k)), gc[...], 0, 0)
            px[k, o, 0] = both[:, :ff].astype(BF)
            px[k, o, 1] = both[:, ff:].astype(BF)

        net.send(("ca", o), px.at[1, o, pl.ds(0, 2)], sb.at[o, pl.ds(0, 2)], sib)

    def weight_b(o):
        @pl.loop(0, 2)
        def _(k):
            px[k, o, 2] = dot(tok_cols(1, shard_of(o, k)), hid[...], 0, 0).astype(BF)

        net.send(("cb", o), px.at[1, o, 2], sb.at[o, 2], sib)

    def add(dst, *srcs):
        total = dst[...].astype(F32)
        for src in srcs:
            total += src[...].astype(F32)
        dst[...] = total.astype(BF)

    def core_a(o):
        net.recv(("ca", o), sb.at[o, pl.ds(0, 2)], sib)

        @pl.loop(0, 2)
        def _(j):
            add(px.at[0, o, j], sb.at[o, j])

    def core_b(o):
        net.recv(("cb", o), sb.at[o, 2], sib)
        add(px.at[0, o, 2], sb.at[o, 2])

    def far_a(s, d):
        net.send(("xh", d, s), px.at[0, s, pl.ds(0, 2), pl.ds(d * half, half), :], xh.at[d, s], x_to[d])

    def near_a(s, d):
        o = 2 + 2 * s + d
        net.recv(("xh", d, s), xh.at[d, s], x_to[1 - d])

        @pl.loop(0, 2)
        def _(j):
            add(px.at[0, o, j, pl.ds(d * half, half), :], xh.at[d, s, j])

        net.send(("xf", d, s), px.at[0, o, pl.ds(0, 2)], xf.at[d, s], x_to[d])

    def last_a(s):
        for d in range(2):
            net.recv(("xf", d, s), xf.at[d, s], x_to[1 - d])

    def cross_a():
        last_a(0)

        @pl.loop(0, 2)
        def _(j):
            add(px.at[0, 6, j], xf.at[0, 0, j], xf.at[1, 0, j])

        net.send("yr", px.at[0, 6, pl.ds(0, 2)], yr, far_y)

    B_OTHER, B_OWN = (0, 2, 3, 6), (1, 4, 5, 7)

    def cross_b(i):
        net.send(("by", i), px.at[0, B_OTHER[i], 2], by.at[i], far_y)

    def crossed_b(i):
        net.recv(("by", i), by.at[i], far_y)
        add(px.at[0, B_OWN[i], 2], by.at[i])

    def far_b(d):
        net.send(("bh", d), px.at[0, 1, 2, pl.ds(d * half, half), :], bh.at[d], x_to[d])

    def near_b(d):
        o = B_OWN[1 + d]
        net.recv(("bh", d), bh.at[d], x_to[1 - d])
        add(px.at[0, o, 2, pl.ds(d * half, half), :], bh.at[d])
        net.send(("bf", d), px.at[0, o, 2], bf.at[d], x_to[d])

    def token_part(q):
        @pl.loop(0, dm // dd // Q)
        def _(i):
            d = q * (dm // dd // Q) + i
            part = dot(gc[:, :ff], w[d, 0], 1, 1) + dot(gc[:, ff:], w[d, 1], 1, 1)
            part = part.reshape(16, rows, dd).astype(BF)
            for n, (l, steps) in enumerate(ARRIVAL):
                gt[q, steps, l, :, columns(i)] = part[n]

    def gt_ref(q, steps):
        return gt.at[q, steps % NZ]

    def z_far(q):
        d = q // 2
        net.send(("z1", d, q % 2), gt_ref(q, 4), z1.at[d, q % 2], z_to[d])

    def z_near(k, q, d):
        ref = gt_ref(q, sign[d] * (3 - k))
        if k > 0:
            net.recv(("zr", d, k - 1, q), zr.at[d, k - 1, q], z_to[1 - d])
            add(ref, zr.at[d, k - 1, q])
        elif q // 2 == d:
            net.recv(("z1", d, q % 2), z1.at[d, q % 2], z_to[1 - d])
            add(ref, z1.at[d, q % 2])
        net.send(("zr", d, k, q), ref, zr.at[d, k, q], z_to[d])

    def z_last(q):
        for d in range(2):
            net.recv(("zr", d, 2, q), zr.at[d, 2, q], z_to[1 - d])
        add(gt.at[q, 0, 1], zr.at[0, 2, q, 1], zr.at[1, 2, q, 1])
        net.send(("lr", q), gt.at[q, 0, 1], lr.at[q], near_y)

    def l_last(q):
        net.recv(("lr", q), lr.at[q], near_y)
        o_tok[:, q * qc:(q + 1) * qc] = (
            gt[q, 0, 0].astype(F32) + zr[0, 2, q, 0].astype(F32)
            + zr[1, 2, q, 0].astype(F32) + lr[q].astype(F32)
        ).astype(BF)

    def end_a():
        last_a(1)
        net.recv("yr", yr, far_y)
        for j, out in enumerate((o_gate, o_up)):
            out[...] = (
                px[0, 7, j].astype(F32) + xf[0, 1, j].astype(F32)
                + xf[1, 1, j].astype(F32) + yr[j].astype(F32)
            ).astype(BF)

    def end_b():
        for d in range(2):
            net.recv(("bf", d), bf.at[d], x_to[1 - d])
        o_down[...] = (
            px[0, 7, 2].astype(F32) + bf[0].astype(F32) + bf[1].astype(F32)
        ).T.astype(BF)

    weight_a(0)
    token_part(2)
    core_a(0)
    z_near(0, 2, 0)
    far_a(0, 1)
    far_a(0, 0)
    z_far(2)
    weight_a(1)
    weight_b(0)
    token_part(0)
    core_b(0)
    cross_b(0)
    z_far(0)
    z_near(0, 0, 1)
    weight_a(2)
    core_a(1)
    far_a(1, 1)
    far_a(1, 0)
    z_near(1, 2, 0)
    z_near(0, 2, 1)
    weight_a(3)
    weight_b(3)
    token_part(3)
    core_b(3)
    z_near(0, 3, 0)
    cross_b(2)
    z_far(3)
    weight_b(1)
    weight_b(2)
    core_a(3)
    near_a(0, 1)
    core_a(2)
    near_a(0, 0)
    z_near(1, 2, 1)
    z_near(0, 0, 0)
    z_near(1, 0, 1)
    weight_b(6)
    weight_b(4)
    weight_b(5)
    core_b(1)
    core_b(2)
    cross_b(1)
    z_near(1, 3, 0)
    weight_a(4)
    token_part(1)
    z_near(0, 3, 1)
    z_near(1, 0, 0)
    z_near(2, 2, 1)
    core_b(6)
    crossed_b(0)
    core_a(4)
    z_far(1)
    cross_b(3)
    weight_a(5)
    weight_a(6)
    z_near(0, 1, 1)
    core_b(5)
    far_b(1)
    far_b(0)
    core_a(5)
    core_b(4)
    core_a(6)
    weight_a(7)
    z_near(2, 0, 0)
    z_near(2, 0, 1)
    cross_a()
    near_a(1, 0)
    crossed_b(2)
    near_a(1, 1)
    z_near(0, 1, 0)
    z_near(2, 2, 0)
    z_near(1, 3, 1)
    near_b(1)
    z_near(1, 1, 0)
    z_near(2, 3, 0)
    z_near(1, 1, 1)
    z_last(0)
    crossed_b(1)
    near_b(0)
    z_last(2)
    core_a(7)
    z_near(2, 3, 1)
    weight_b(7)
    z_near(2, 1, 0)
    z_near(2, 1, 1)
    end_a()
    z_last(3)
    core_b(7)
    crossed_b(3)
    l_last(0)
    z_last(1)
    l_last(2)
    l_last(3)
    end_b()
    l_last(1)
    net.finish()
    assert len(net.index) <= N_COPIES


def local(tokens, grad_out, gate_weight, up_weight, down_weight):
    rows, dm = tokens.shape
    dd, ff = gate_weight.shape
    qc = dm // Q
    any_space = pl.BlockSpec(memory_space=pl.ANY)
    in_vmem = pl.BlockSpec(memory_space=pltpu.VMEM)
    return pl.pallas_call(
        kernel,
        out_shape=(
            jax.ShapeDtypeStruct((rows, dm), BF),
            jax.ShapeDtypeStruct((dd, ff), BF),
            jax.ShapeDtypeStruct((dd, ff), BF),
            jax.ShapeDtypeStruct((ff, dd), BF),
        ),
        in_specs=[any_space] * 5,
        out_specs=[in_vmem] * 4,
        scratch_shapes=[
            pltpu.VMEM((16, 2, rows, dm), BF),
            pltpu.VMEM((16, 3, dd, ff), BF),
            pltpu.VMEM((3, 16 * rows, ff), F32),
            pltpu.VMEM((16 * rows, 2 * ff), BF),
            pltpu.VMEM((16 * rows, ff), BF),
            pltpu.VMEM((2, 8, 3, dd, ff), BF),
            pltpu.VMEM((8, 3, dd, ff), BF),
            pltpu.VMEM((2, 2, 2, dd // 2, ff), BF),
            pltpu.VMEM((2, 2, 2, dd, ff), BF),
            pltpu.VMEM((2, dd, ff), BF),
            pltpu.VMEM((2, dd // 2, ff), BF),
            pltpu.VMEM((2, dd, ff), BF),
            pltpu.VMEM((4, dd, ff), BF),
            pltpu.VMEM((Q, NZ, 2, rows, qc), BF),
            pltpu.VMEM((2, 2, 2, rows, qc), BF),
            pltpu.VMEM((2, 3, Q, 2, rows, qc), BF),
            pltpu.VMEM((Q, rows, qc), BF),
            pltpu.VMEM((ff, dd), BF),
            pltpu.SemaphoreType.DMA((N_COPIES,)),
            pltpu.SemaphoreType.DMA((N_COPIES,)),
            pltpu.SemaphoreType.DMA((5,)),
        ],
        compiler_params=pltpu.CompilerParams(
            collective_id=0, has_side_effects=True, vmem_limit_bytes=63 * 1024 * 1024
        ),
    )(tokens, grad_out, gate_weight, up_weight, down_weight)


def solution(mesh):
    return jax.shard_map(
        local,
        mesh=mesh,
        in_specs=(
            P(("dp", "tensor"), None),
            P(("dp", "tensor"), None),
            P("dp", "tensor"),
            P("dp", "tensor"),
            P("tensor", "dp"),
        ),
        out_specs=(
            P(("dp", "tensor"), None),
            P("dp", "tensor"),
            P("dp", "tensor"),
            P("tensor", "dp"),
        ),
        check_vma=False,
    )
```

```python
import jax
import jax.numpy as jnp
from jax import lax
from jax.experimental import pallas as pl
from jax.experimental.pallas import tpu as pltpu
from jax.sharding import PartitionSpec as P

MESH = pl.DeviceIdType.MESH
BF, F32 = jnp.bfloat16, jnp.float32
NX, NZ = 4, 8
Q = 4


class Links:
    def __init__(self, send_sem, recv_sem):
        self.send_sem, self.recv_sem = send_sem, recv_sem
        self.index, self.sent = {}, []

    def at(self, name):
        return self.index.setdefault(name, len(self.index))

    def send(self, name, src, dst, device):
        i = self.at(name)
        copy = pltpu.make_async_remote_copy(
            src_ref=src, dst_ref=dst, send_sem=self.send_sem.at[i], recv_sem=self.recv_sem.at[i],
            device_id=device, device_id_type=MESH,
        )
        copy.start()
        self.sent.append(copy)

    def recv(self, name, ref, device):
        i = self.at(name)
        pltpu.make_async_remote_copy(
            src_ref=ref, dst_ref=ref, send_sem=self.send_sem.at[i], recv_sem=self.recv_sem.at[i],
            device_id=device, device_id_type=MESH,
        ).wait_recv()

    def finish(self):
        for copy in self.sent:
            copy.wait_send()


N_COPIES = 160


def dot(a, b, ca, cb):
    return lax.dot_general(a, b, (((ca,), (cb,)), ((), ())), preferred_element_type=F32)


ARRIVAL = ((0, 0), (0, 1), (0, 7), (0, 2), (0, 6), (0, 3), (0, 5), (0, 4),
           (1, 1), (1, 7), (1, 2), (1, 6), (1, 4), (1, 3), (1, 5), (1, 0))
PLACE = {shard: i for i, shard in enumerate(ARRIVAL)}
EARLY = 10
ORDER = ((2, 1), (2, 0), (1, 1), (3, 1), (1, 0), (3, 0), (0, 1), (0, 0))


def kernel(tok, grd, gw, uw, dw, o_tok, o_gate, o_up, o_down,
           tg, w, acc, gc, hid, px, sb, xh, xf, yr, bh, bf, by, gt, z1, zr, lr, dws, s_tok, s_w,
           send_sem, recv_sem, local_sem, out_sem):
    rows, dm = tok.shape
    dd, ff = gw.shape
    half = dd // 2
    qc = dm // Q
    dp, ten = lax.axis_index("dp"), lax.axis_index("tensor")
    yh, x, c = dp // 8, (dp // 2) % NX, dp % 2
    z, yl = ten // 2, ten % 2

    def dp_at(h, xx, cc):
        return h * 8 + (xx % NX) * 2 + cc

    def ten_at(zz, ll):
        return (zz % NZ) * 2 + ll

    oh, ol, oc = 1 - yh, 1 - yl, 1 - c
    sib = {"dp": dp_at(yh, x, oc)}
    far_y = {"dp": dp_at(oh, x, c)}
    x_to = ({"dp": dp_at(yh, x + 1, c)}, {"dp": dp_at(yh, x + NX - 1, c)})
    near_y = {"tensor": ten_at(z, ol)}
    z_to = ({"tensor": ten_at(z + 1, yl)}, {"tensor": ten_at(z + NZ - 1, yl)})
    peers = (sib, far_y, *x_to, near_y, *z_to)

    me_w = dp
    locals_ = [
        pltpu.make_async_copy(src, dst, local_sem.at[i])
        for i, (src, dst) in enumerate((
            (tok, tg.at[0, 0]), (grd, tg.at[0, 1]),
            (gw, w.at[me_w, 0]), (uw, w.at[me_w, 1]), (dw, dws),
        ))
    ]
    for copy in locals_:
        copy.start()
    barrier = pltpu.get_barrier_semaphore()
    for peer in peers:
        pl.semaphore_signal(barrier, inc=1, device_id=peer, device_id_type=MESH)
    pl.semaphore_wait(barrier, len(peers))

    net = Links(send_sem, recv_sem)
    sign = (1, -1)

    def t_ref(l, steps, part=None):
        place = PLACE[l, steps % NZ]
        return tg.at[place] if part is None else tg.at[place, part]

    def z_send(l, k, part):
        for d in range(2):
            if k < 3 or part == d:
                net.send(("z", d, k, l, part), t_ref(l, -sign[d] * k, part), t_ref(l, -sign[d] * (k + 1), part), z_to[d])

    def z_recv(l, k, part):
        for d in range(2):
            if k < 4 or part == d:
                net.recv(("z", d, k - 1, l, part), t_ref(l, -sign[d] * k, part), z_to[1 - d])

    def z_pass(l, k):
        for part in range(2):
            z_recv(l, k, part)
            z_send(l, k, part)

    def l_send(part, *steps):
        for k in steps:
            net.send(("l", k, part), t_ref(0, k, part), t_ref(1, k, part), near_y)

    def l_recv(part, *steps):
        for k in steps:
            net.recv(("l", k, part), t_ref(1, k, part), near_y)

    def w_ref(slot, part):
        return w.at[slot] if part is None else w.at[slot, :, pl.ds(part * half, half), :]

    def w_send(name, slot, device, part=None):
        net.send(name, w_ref(slot, part), w_ref(slot, part), device)

    def w_recv(name, slot, device, part=None):
        net.recv(name, w_ref(slot, part), device)

    def x_slot(h, d, k, core):
        return dp_at(yh if h == 0 else oh, x + NX - sign[d] * k, core)

    def x_start(h):
        for d in range(2):
            w_send(("x", d, 0, h), x_slot(h, d, 0, c), x_to[d])

    def x_pass(h):
        for d in range(2):
            w_recv(("x", d, 0, h), x_slot(h, d, 1, c), x_to[1 - d])
            w_send(("x", d, 1, h), x_slot(h, d, 1, c), x_to[d], d)
            w_send(("sib", d, 1, h), x_slot(h, d, 1, c), sib)

    def x_end(h):
        for d in range(2):
            w_recv(("x", d, 1, h), x_slot(h, d, 2, c), x_to[1 - d], d)
            w_send(("sib", d, 2, h), x_slot(h, d, 2, c), sib, d)

    def ag_head():
        for part in range(2):
            locals_[part].wait()
            z_send(0, 0, part)
        for copy in locals_[2:]:
            copy.wait()
        first = w.at[me_w, pl.ds(0, 2)]
        net.send(("yh", 0), first, first, far_y)
        w[me_w, 2] = dws[...].T
        x_start(0)
        net.send(("yh", 1), w.at[me_w, 2], w.at[me_w, 2], far_y)
        w_send(("sib", 0, 0, 0), me_w, sib)
        acc[...] = jnp.zeros_like(acc)

    def sib_recv(h):
        w_recv(("sib", 0, 0, h), x_slot(h, 0, 0, oc), sib)
        for d in range(2):
            w_recv(("sib", d, 1, h), x_slot(h, d, 1, oc), sib)

    def sib_end(h):
        for d in range(2):
            w_recv(("sib", d, 2, h), x_slot(h, d, 2, oc), sib, d)

    def columns(d):
        return pl.ds(pl.multiple_of(d * dd, dd), dd)

    def tok_cols(part, d, first=0, end=16):
        return tg[first:end, part, :, columns(d)].reshape((end - first) * rows, dd)

    def fwd(first, end, begin, stop, parts):
        r = pl.ds(first * rows, (end - first) * rows)

        @pl.loop(begin, stop)
        def _(pair):
            d = dp_at((yh + pair // 4) % 2, x + pair % 4 + 3, 0)
            both = pl.ds(pl.multiple_of(d * dd, 2 * dd), 2 * dd)

            def product(part, weight):
                a = tg[first:end, part, :, both].reshape((end - first) * rows, 2 * dd)
                return dot(a, w[pl.ds(d, 2), weight].reshape(2 * dd, ff), 1, 0)

            if 0 in parts:
                acc[0, r] += product(0, 0)
                acc[1, r] += product(0, 1)
            if 1 in parts:
                acc[2, r] += product(1, 2)

    def fwd_late(part):
        r = pl.ds(EARLY * rows, (16 - EARLY) * rows)

        @pl.loop(0, 4)
        def _(i):
            four = pl.ds(pl.multiple_of(i * 4 * dd, 4 * dd), 4 * dd)
            a = tg[EARLY:16, part, :, four].reshape((16 - EARLY) * rows, 4 * dd)
            for weight in ((0, 1), (2,))[part]:
                acc[weight, r] += dot(a, w[pl.ds(i * 4, 4), weight].reshape(4 * dd, ff), 1, 0)

    def hidden(first, end):
        @pl.loop(first, end)
        def _(i):
            r = pl.ds(pl.multiple_of(i * rows, rows), rows)
            gate, up = acc[0, r], acc[1, r]
            hid[r] = (gate * (1.0 / (1.0 + jnp.exp(-gate))) * up).astype(BF)

    def grads(first, end):
        @pl.loop(first, end)
        def _(i):
            r = pl.ds(pl.multiple_of(i * rows, rows), rows)
            gate, up, grad_hidden = acc[0, r], acc[1, r], acc[2, r]
            sigmoid = 1.0 / (1.0 + jnp.exp(-gate))
            activated = gate * sigmoid
            gc[r, :ff] = (grad_hidden * up * sigmoid * (1.0 + gate * (1.0 - sigmoid))).astype(BF)
            gc[r, ff:] = (grad_hidden * activated).astype(BF)

    ag_head()
    z_pass(0, 1)
    l_send(0, 1, 7)
    l_send(1, 1, 7)
    l_send(0, 0)
    x_pass(0)
    other = x_slot(1, 0, 0, c)
    net.recv(("yh", 0), w.at[other, pl.ds(0, 2)], far_y)
    net.recv(("yh", 1), w.at[other, 2], far_y)
    x_start(1)
    w_send(("sib", 0, 0, 1), other, sib)
    z_pass(0, 2)
    z_pass(0, 3)
    l_recv(0, 1, 7)
    z_send(1, 1, 0)
    x_end(0)
    l_recv(1, 1, 7)
    z_send(1, 1, 1)
    z_recv(0, 4, 0)
    l_send(0, 4)
    l_send(1, 0)
    z_recv(0, 4, 1)
    l_send(1, 4)
    sib_recv(0)
    sib_end(0)
    fwd(0, EARLY, 0, 2, (0, 1))
    x_pass(1)
    fwd(0, EARLY, 2, 4, (0, 1))
    z_recv(1, 2, 0)
    z_send(1, 2, 0)
    sib_recv(1)
    fwd(0, EARLY, 4, 7, (0, 1))
    x_end(1)
    z_recv(1, 2, 1)
    z_send(1, 2, 1)
    sib_end(1)
    fwd(0, EARLY, 7, 8, (0, 1))
    hidden(0, EARLY)
    grads(0, EARLY)

    def late(part):
        l_recv(part, 0, 4)
        z_recv(1, 3, part)

    late(0)
    fwd_late(0)
    hidden(EARLY, 16)
    late(1)

    def grad_h():
        fwd_late(1)
        grads(EARLY, 16)

    def shard_of(o, k):
        steps, h = ORDER[o]
        return dp_at(yh if h == 0 else oh, x + steps, lax.rem(c + k, 2))

    def weight_a(o):
        for k in (1, 0):
            both = dot(tok_cols(0, shard_of(o, k)), gc[...], 0, 0)
            px[k, o, 0] = both[:, :ff].astype(BF)
            px[k, o, 1] = both[:, ff:].astype(BF)
            if k == 1:
                net.send(("ca", o), px.at[1, o, pl.ds(0, 2)], sb.at[o, pl.ds(0, 2)], sib)

    def weight_b(o):
        for k in (1, 0):
            px[k, o, 2] = dot(tok_cols(1, shard_of(o, k)), hid[...], 0, 0).astype(BF)
            if k == 1:
                net.send(("cb", o), px.at[1, o, 2], sb.at[o, 2], sib)

    def add(dst, *srcs):
        total = dst[...].astype(F32)
        for src in srcs:
            total += src[...].astype(F32)
        dst[...] = total.astype(BF)

    def core_a(o):
        net.recv(("ca", o), sb.at[o, pl.ds(0, 2)], sib)

        @pl.loop(0, 2)
        def _(j):
            add(px.at[0, o, j], sb.at[o, j])

    def core_b(o):
        net.recv(("cb", o), sb.at[o, 2], sib)
        add(px.at[0, o, 2], sb.at[o, 2])

    def far_a(s, d, j):
        net.send(("xh", d, s, j), px.at[0, s, j, pl.ds(d * half, half), :], xh.at[d, s, j], x_to[d])

    def near_a(s, d, j):
        o = 2 + 2 * s + d
        net.recv(("xh", d, s, j), xh.at[d, s, j], x_to[1 - d])
        add(px.at[0, o, j, pl.ds(d * half, half), :], xh.at[d, s, j])
        net.send(("xf", d, s, j), px.at[0, o, j], xf.at[d, s, j], x_to[d])

    def last_a(s, j):
        for d in range(2):
            net.recv(("xf", d, s, j), xf.at[d, s, j], x_to[1 - d])

    def cross_a(j):
        last_a(0, j)
        add(px.at[0, 6, j], xf.at[0, 0, j], xf.at[1, 0, j])
        net.send(("yr", j), px.at[0, 6, j], yr.at[j], far_y)

    B_OTHER, B_OWN = (0, 2, 3, 6), (1, 4, 5, 7)

    def cross_b(i):
        net.send(("by", i), px.at[0, B_OTHER[i], 2], by.at[i], far_y)

    def crossed_b(i):
        net.recv(("by", i), by.at[i], far_y)
        add(px.at[0, B_OWN[i], 2], by.at[i])

    def far_b(d):
        net.send(("bh", d), px.at[0, 1, 2, pl.ds(d * half, half), :], bh.at[d], x_to[d])

    def near_b(d):
        o = B_OWN[1 + d]
        net.recv(("bh", d), bh.at[d], x_to[1 - d])
        add(px.at[0, o, 2, pl.ds(d * half, half), :], bh.at[d])
        net.send(("bf", d), px.at[0, o, 2], bf.at[d], x_to[d])

    def token_part(q):
        @pl.loop(0, dm // dd // Q)
        def _(i):
            d = q * (dm // dd // Q) + i
            part = dot(gc[:, :ff], w[d, 0], 1, 1) + dot(gc[:, ff:], w[d, 1], 1, 1)
            part = part.reshape(16, rows, dd).astype(BF)
            for n, (l, steps) in enumerate(ARRIVAL):
                gt[q, steps, l, :, columns(i)] = part[n]

    def gt_ref(q, steps):
        return gt.at[q, steps % NZ]

    def z_far(q):
        d = q // 2
        net.send(("z1", d, q % 2), gt_ref(q, 4), z1.at[d, q % 2], z_to[d])

    def z_near(k, q, d):
        ref = gt_ref(q, sign[d] * (3 - k))
        if k > 0:
            net.recv(("zr", d, k - 1, q), zr.at[d, k - 1, q], z_to[1 - d])
            add(ref, zr.at[d, k - 1, q])
        elif q // 2 == d:
            net.recv(("z1", d, q % 2), z1.at[d, q % 2], z_to[1 - d])
            add(ref, z1.at[d, q % 2])
        net.send(("zr", d, k, q), ref, zr.at[d, k, q], z_to[d])

    def z_last(q):
        for d in range(2):
            net.recv(("zr", d, 2, q), zr.at[d, 2, q], z_to[1 - d])
        add(gt.at[q, 0, 1], zr.at[0, 2, q, 1], zr.at[1, 2, q, 1])
        net.send(("lr", q), gt.at[q, 0, 1], lr.at[q], near_y)

    done = []

    def write(src, dst):
        copy = pltpu.make_async_copy(src, dst, out_sem.at[len(done)])
        copy.start()
        done.append(copy)

    def l_last(q):
        net.recv(("lr", q), lr.at[q], near_y)
        part = pl.ds(q * qc, qc)
        s_tok[:, part] = (
            gt[q, 0, 0].astype(F32) + zr[0, 2, q, 0].astype(F32)
            + zr[1, 2, q, 0].astype(F32) + lr[q].astype(F32)
        ).astype(BF)
        write(s_tok.at[:, part], o_tok.at[:, part])

    def end_a(j):
        last_a(1, j)
        net.recv(("yr", j), yr.at[j], far_y)
        s_w[j] = (
            px[0, 7, j].astype(F32) + xf[0, 1, j].astype(F32)
            + xf[1, 1, j].astype(F32) + yr[j].astype(F32)
        ).astype(BF)
        write(s_w.at[j], (o_gate, o_up)[j])

    def end_b():
        for d in range(2):
            net.recv(("bf", d), bf.at[d], x_to[1 - d])
        dws[...] = (
            px[0, 7, 2].astype(F32) + bf[0].astype(F32) + bf[1].astype(F32)
        ).T.astype(BF)
        write(dws, o_down)

    grad_h()
    weight_a(0)
    token_part(2)
    core_a(0)
    z_near(0, 2, 0)
    far_a(0, 1, 0)
    far_a(0, 1, 1)
    far_a(0, 0, 0)
    far_a(0, 0, 1)
    z_far(2)
    weight_a(1)
    weight_b(0)
    token_part(0)
    core_b(0)
    cross_b(0)
    z_far(0)
    z_near(0, 0, 1)
    weight_a(2)
    core_a(1)
    far_a(1, 1, 0)
    far_a(1, 1, 1)
    far_a(1, 0, 0)
    far_a(1, 0, 1)
    z_near(1, 2, 0)
    z_near(0, 2, 1)
    weight_a(3)
    weight_b(3)
    token_part(3)
    core_b(3)
    z_near(0, 3, 0)
    cross_b(2)
    z_far(3)
    weight_b(1)
    weight_b(2)
    core_a(3)
    near_a(0, 1, 0)
    near_a(0, 1, 1)
    core_a(2)
    near_a(0, 0, 0)
    near_a(0, 0, 1)
    z_near(1, 2, 1)
    z_near(0, 0, 0)
    z_near(1, 0, 1)
    weight_b(6)
    weight_b(4)
    weight_b(5)
    core_b(1)
    core_b(2)
    cross_b(1)
    z_near(1, 3, 0)
    weight_a(4)
    token_part(1)
    z_near(0, 3, 1)
    z_near(1, 0, 0)
    z_near(2, 2, 1)
    core_b(6)
    crossed_b(0)
    core_a(4)
    z_far(1)
    cross_b(3)
    weight_a(5)
    weight_a(6)
    z_near(0, 1, 1)
    core_b(5)
    far_b(1)
    far_b(0)
    core_a(5)
    core_b(4)
    core_a(6)
    weight_a(7)
    z_near(2, 0, 0)
    z_near(2, 0, 1)
    cross_a(0)
    cross_a(1)
    near_a(1, 0, 0)
    near_a(1, 0, 1)
    crossed_b(2)
    near_a(1, 1, 0)
    near_a(1, 1, 1)
    z_near(0, 1, 0)
    z_near(2, 2, 0)
    z_near(1, 3, 1)
    near_b(1)
    z_near(1, 1, 0)
    z_near(2, 3, 0)
    z_near(1, 1, 1)
    z_last(0)
    crossed_b(1)
    near_b(0)
    z_last(2)
    core_a(7)
    z_near(2, 3, 1)
    weight_b(7)
    z_near(2, 1, 0)
    z_near(2, 1, 1)
    end_a(0)
    end_a(1)
    z_last(3)
    core_b(7)
    crossed_b(3)
    l_last(0)
    z_last(1)
    l_last(2)
    l_last(3)
    end_b()
    l_last(1)
    for copy in done:
        copy.wait()
    net.finish()
    assert len(net.index) <= N_COPIES


def deliver(a, b, c, d, to_a, to_b, to_c, to_d):
    for src, dst in ((a, to_a), (b, to_b), (c, to_c), (d, to_d)):
        dst[...] = src[...]


def local(tokens, grad_out, gate_weight, up_weight, down_weight):
    rows, dm = tokens.shape
    dd, ff = gate_weight.shape
    qc = dm // Q
    any_space = pl.BlockSpec(memory_space=pl.ANY)
    out = pl.pallas_call(
        kernel,
        out_shape=(
            jax.ShapeDtypeStruct((rows, dm), BF),
            jax.ShapeDtypeStruct((dd, ff), BF),
            jax.ShapeDtypeStruct((dd, ff), BF),
            jax.ShapeDtypeStruct((ff, dd), BF),
        ),
        in_specs=[any_space] * 5,
        out_specs=[any_space] * 4,
        scratch_shapes=[
            pltpu.VMEM((16, 2, rows, dm), BF),
            pltpu.VMEM((16, 3, dd, ff), BF),
            pltpu.VMEM((3, 16 * rows, ff), F32),
            pltpu.VMEM((16 * rows, 2 * ff), BF),
            pltpu.VMEM((16 * rows, ff), BF),
            pltpu.VMEM((2, 8, 3, dd, ff), BF),
            pltpu.VMEM((8, 3, dd, ff), BF),
            pltpu.VMEM((2, 2, 2, dd // 2, ff), BF),
            pltpu.VMEM((2, 2, 2, dd, ff), BF),
            pltpu.VMEM((2, dd, ff), BF),
            pltpu.VMEM((2, dd // 2, ff), BF),
            pltpu.VMEM((2, dd, ff), BF),
            pltpu.VMEM((4, dd, ff), BF),
            pltpu.VMEM((Q, NZ, 2, rows, qc), BF),
            pltpu.VMEM((2, 2, 2, rows, qc), BF),
            pltpu.VMEM((2, 3, Q, 2, rows, qc), BF),
            pltpu.VMEM((Q, rows, qc), BF),
            pltpu.VMEM((ff, dd), BF),
            pltpu.VMEM((rows, dm), BF),
            pltpu.VMEM((2, dd, ff), BF),
            pltpu.SemaphoreType.DMA((N_COPIES,)),
            pltpu.SemaphoreType.DMA((N_COPIES,)),
            pltpu.SemaphoreType.DMA((5,)),
            pltpu.SemaphoreType.DMA((7,)),
        ],
        compiler_params=pltpu.CompilerParams(
            collective_id=0, has_side_effects=True, vmem_limit_bytes=63 * 1024 * 1024
        ),
    )(tokens, grad_out, gate_weight, up_weight, down_weight)
    return pl.pallas_call(
        deliver,
        out_shape=tuple(jax.ShapeDtypeStruct(a.shape, BF) for a in out),
        in_specs=[pl.BlockSpec(memory_space=pltpu.VMEM)] * 4,
        out_specs=[pl.BlockSpec(memory_space=pltpu.VMEM)] * 4,
        compiler_params=pltpu.CompilerParams(vmem_limit_bytes=63 * 1024 * 1024),
    )(*out)


def solution(mesh):
    return jax.shard_map(
        local,
        mesh=mesh,
        in_specs=(
            P(("dp", "tensor"), None),
            P(("dp", "tensor"), None),
            P("dp", "tensor"),
            P("dp", "tensor"),
            P("tensor", "dp"),
        ),
        out_specs=(
            P(("dp", "tensor"), None),
            P("dp", "tensor"),
            P("dp", "tensor"),
            P("tensor", "dp"),
        ),
        check_vma=False,
    )
```

```python
import jax
import jax.numpy as jnp
from jax import lax
from jax.experimental import pallas as pl
from jax.experimental.pallas import tpu as pltpu
from jax.sharding import PartitionSpec as P

MESH = pl.DeviceIdType.MESH
BF, F32 = jnp.bfloat16, jnp.float32
NX, NZ = 4, 8
Q = 4


class Links:
    def __init__(self, send_sem, recv_sem):
        self.send_sem, self.recv_sem = send_sem, recv_sem
        self.index, self.sent = {}, []

    def at(self, name):
        return self.index.setdefault(name, len(self.index))

    def send(self, name, src, dst, device):
        i = self.at(name)
        copy = pltpu.make_async_remote_copy(
            src_ref=src, dst_ref=dst, send_sem=self.send_sem.at[i], recv_sem=self.recv_sem.at[i],
            device_id=device, device_id_type=MESH,
        )
        copy.start()
        self.sent.append(copy)

    def recv(self, name, ref, device):
        i = self.at(name)
        pltpu.make_async_remote_copy(
            src_ref=ref, dst_ref=ref, send_sem=self.send_sem.at[i], recv_sem=self.recv_sem.at[i],
            device_id=device, device_id_type=MESH,
        ).wait_recv()

    def finish(self):
        for copy in self.sent:
            copy.wait_send()


N_COPIES = 192


def dot(a, b, ca, cb):
    return lax.dot_general(a, b, (((ca,), (cb,)), ((), ())), preferred_element_type=F32)


ARRIVAL = ((0, 0), (0, 1), (0, 7), (0, 2), (0, 6), (0, 3), (0, 5), (0, 4),
           (1, 1), (1, 7), (1, 2), (1, 6), (1, 4), (1, 3), (1, 5), (1, 0))
PLACE = {shard: i for i, shard in enumerate(ARRIVAL)}
EARLY = 10
ORDER = ((2, 1), (2, 0), (1, 1), (3, 1), (1, 0), (3, 0), (0, 1), (0, 0))


def kernel(tok, grd, gw, uw, dw, o_tok, o_gate, o_up, o_down,
           tg, w, acc, gc, hid, px, sb, xh, xf, yr, bh, bf, by, gt, z1, zr, lr, dws, s_tok, s_w,
           send_sem, recv_sem, local_sem, out_sem):
    rows, dm = tok.shape
    dd, ff = gw.shape
    half = dd // 2
    qc = dm // Q
    dp, ten = lax.axis_index("dp"), lax.axis_index("tensor")
    yh, x, c = dp // 8, (dp // 2) % NX, dp % 2
    z, yl = ten // 2, ten % 2

    def dp_at(h, xx, cc):
        return h * 8 + (xx % NX) * 2 + cc

    def ten_at(zz, ll):
        return (zz % NZ) * 2 + ll

    oh, ol, oc = 1 - yh, 1 - yl, 1 - c
    sib = {"dp": dp_at(yh, x, oc)}
    far_y = {"dp": dp_at(oh, x, c)}
    x_to = ({"dp": dp_at(yh, x + 1, c)}, {"dp": dp_at(yh, x + NX - 1, c)})
    near_y = {"tensor": ten_at(z, ol)}
    z_to = ({"tensor": ten_at(z + 1, yl)}, {"tensor": ten_at(z + NZ - 1, yl)})
    peers = (sib, far_y, *x_to, near_y, *z_to)

    me_w = dp
    locals_ = [
        pltpu.make_async_copy(src, dst, local_sem.at[i])
        for i, (src, dst) in enumerate((
            (tok, tg.at[0, 0]), (grd, tg.at[0, 1]),
            (gw, w.at[me_w, 0]), (uw, w.at[me_w, 1]), (dw, dws),
        ))
    ]
    for copy in locals_:
        copy.start()
    barrier = pltpu.get_barrier_semaphore()
    for peer in peers:
        pl.semaphore_signal(barrier, inc=1, device_id=peer, device_id_type=MESH)
    pl.semaphore_wait(barrier, len(peers))

    net = Links(send_sem, recv_sem)
    sign = (1, -1)

    def t_ref(l, steps, part=None):
        place = PLACE[l, steps % NZ]
        return tg.at[place] if part is None else tg.at[place, part]

    def z_send(l, k, part):
        for d in range(2):
            if k < 3 or part == d:
                net.send(("z", d, k, l, part), t_ref(l, -sign[d] * k, part), t_ref(l, -sign[d] * (k + 1), part), z_to[d])

    def z_recv(l, k, part):
        for d in range(2):
            if k < 4 or part == d:
                net.recv(("z", d, k - 1, l, part), t_ref(l, -sign[d] * k, part), z_to[1 - d])

    def z_pass(l, k):
        for part in range(2):
            z_recv(l, k, part)
            z_send(l, k, part)

    def l_send(part, *steps):
        for k in steps:
            net.send(("l", k, part), t_ref(0, k, part), t_ref(1, k, part), near_y)

    def l_recv(part, *steps):
        for k in steps:
            net.recv(("l", k, part), t_ref(1, k, part), near_y)

    def w_ref(slot, part):
        return w.at[slot] if part is None else w.at[slot, :, pl.ds(part * half, half), :]

    def w_send(name, slot, device, part=None):
        net.send(name, w_ref(slot, part), w_ref(slot, part), device)

    def w_recv(name, slot, device, part=None):
        net.recv(name, w_ref(slot, part), device)

    def x_slot(h, d, k, core):
        return dp_at(yh if h == 0 else oh, x + NX - sign[d] * k, core)

    def x_start(h):
        for d in range(2):
            w_send(("x", d, 0, h), x_slot(h, d, 0, c), x_to[d])

    def x_pass(h):
        for d in range(2):
            w_recv(("x", d, 0, h), x_slot(h, d, 1, c), x_to[1 - d])
            w_send(("x", d, 1, h), x_slot(h, d, 1, c), x_to[d], d)
            w_send(("sib", d, 1, h), x_slot(h, d, 1, c), sib)

    def x_end(h):
        for d in range(2):
            w_recv(("x", d, 1, h), x_slot(h, d, 2, c), x_to[1 - d], d)
            w_send(("sib", d, 2, h), x_slot(h, d, 2, c), sib, d)

    def ag_head():
        for part in range(2):
            locals_[part].wait()
            z_send(0, 0, part)
        for copy in locals_[2:]:
            copy.wait()
        first = w.at[me_w, pl.ds(0, 2)]
        net.send(("yh", 0), first, first, far_y)
        w[me_w, 2] = dws[...].T
        x_start(0)
        net.send(("yh", 1), w.at[me_w, 2], w.at[me_w, 2], far_y)
        w_send(("sib", 0, 0, 0), me_w, sib)
        acc[...] = jnp.zeros_like(acc)

    def sib_recv(h):
        w_recv(("sib", 0, 0, h), x_slot(h, 0, 0, oc), sib)
        for d in range(2):
            w_recv(("sib", d, 1, h), x_slot(h, d, 1, oc), sib)

    def sib_end(h):
        for d in range(2):
            w_recv(("sib", d, 2, h), x_slot(h, d, 2, oc), sib, d)

    def columns(d):
        return pl.ds(pl.multiple_of(d * dd, dd), dd)

    def tok_cols(part, d, first=0, end=16):
        return tg[first:end, part, :, columns(d)].reshape((end - first) * rows, dd)

    def fwd(first, end, begin, stop, parts):
        r = pl.ds(first * rows, (end - first) * rows)

        @pl.loop(begin, stop)
        def _(pair):
            d = dp_at((yh + pair // 4) % 2, x + pair % 4 + 3, 0)
            both = pl.ds(pl.multiple_of(d * dd, 2 * dd), 2 * dd)

            def product(part, weight):
                a = tg[first:end, part, :, both].reshape((end - first) * rows, 2 * dd)
                return dot(a, w[pl.ds(d, 2), weight].reshape(2 * dd, ff), 1, 0)

            if 0 in parts:
                acc[0, r] += product(0, 0)
                acc[1, r] += product(0, 1)
            if 1 in parts:
                acc[2, r] += product(1, 2)

    def fwd_late(part, begin=0, stop=4):
        r = pl.ds(EARLY * rows, (16 - EARLY) * rows)

        @pl.loop(begin, stop)
        def _(i):
            four = pl.ds(pl.multiple_of(i * 4 * dd, 4 * dd), 4 * dd)
            a = tg[EARLY:16, part, :, four].reshape((16 - EARLY) * rows, 4 * dd)
            for weight in ((0, 1), (2,))[part]:
                acc[weight, r] += dot(a, w[pl.ds(i * 4, 4), weight].reshape(4 * dd, ff), 1, 0)

    def hidden(first, end):
        @pl.loop(first, end)
        def _(i):
            r = pl.ds(pl.multiple_of(i * rows, rows), rows)
            gate, up = acc[0, r], acc[1, r]
            sigmoid = 1.0 / (1.0 + jnp.exp(-gate))
            activated = gate * sigmoid
            hid[r] = (activated * up).astype(BF)
            acc[0, r] = up * sigmoid * (1.0 + gate * (1.0 - sigmoid))
            acc[1, r] = activated

    def grads(first, end):
        @pl.loop(first, end)
        def _(i):
            r = pl.ds(pl.multiple_of(i * rows, rows), rows)
            grad_hidden = acc[2, r]
            gc[r, :ff] = (grad_hidden * acc[0, r]).astype(BF)
            gc[r, ff:] = (grad_hidden * acc[1, r]).astype(BF)

    def last_ref(steps, h):
        return tg.at[PLACE[1, steps % NZ], 1, :, pl.ds(h * (dm // 2), dm // 2)]

    def last_send():
        for h in range(2):
            for d in range(2):
                net.send(("z", d, 2, 1, 1, h), last_ref(-2 * sign[d], h), last_ref(-3 * sign[d], h), z_to[d])

    def last_recv(h):
        for d in range(2):
            net.recv(("z", d, 2, 1, 1, h), last_ref(-3 * sign[d], h), z_to[1 - d])

    ag_head()
    z_pass(0, 1)
    l_send(0, 1, 7)
    l_send(1, 1, 7)
    l_send(0, 0)
    x_pass(0)
    other = x_slot(1, 0, 0, c)
    net.recv(("yh", 0), w.at[other, pl.ds(0, 2)], far_y)
    net.recv(("yh", 1), w.at[other, 2], far_y)
    x_start(1)
    w_send(("sib", 0, 0, 1), other, sib)
    z_pass(0, 2)
    z_pass(0, 3)
    l_recv(0, 1, 7)
    z_send(1, 1, 0)
    x_end(0)
    l_recv(1, 1, 7)
    z_send(1, 1, 1)
    z_recv(0, 4, 0)
    l_send(0, 4)
    l_send(1, 0)
    z_recv(0, 4, 1)
    l_send(1, 4)
    sib_recv(0)
    sib_end(0)
    fwd(0, EARLY, 0, 2, (0, 1))
    x_pass(1)
    fwd(0, EARLY, 2, 4, (0, 1))
    z_recv(1, 2, 0)
    z_send(1, 2, 0)
    sib_recv(1)
    fwd(0, EARLY, 4, 7, (0, 1))
    x_end(1)
    z_recv(1, 2, 1)
    last_send()
    sib_end(1)
    fwd(0, EARLY, 7, 8, (0, 1))
    hidden(0, EARLY)
    grads(0, EARLY)

    l_recv(0, 0, 4)
    z_recv(1, 3, 0)
    fwd_late(0)
    hidden(EARLY, 16)
    l_recv(1, 0, 4)
    last_recv(0)
    fwd_late(1, 0, 2)
    last_recv(1)

    def grad_h():
        fwd_late(1, 2, 4)
        grads(EARLY, 16)

    def shard_of(o, k):
        steps, h = ORDER[o]
        return dp_at(yh if h == 0 else oh, x + steps, lax.rem(c + k, 2))

    def send_a(o):
        a = tok_cols(0, shard_of(o, 1))
        for j in range(2):
            px[1, o, j] = dot(a, gc[:, j * ff:(j + 1) * ff], 0, 0).astype(BF)
            net.send(("ca", o, j), px.at[1, o, j], sb.at[o, j], sib)

    def own_a(o):
        both = dot(tok_cols(0, shard_of(o, 0)), gc[...], 0, 0)
        px[0, o, 0] = both[:, :ff].astype(BF)
        px[0, o, 1] = both[:, ff:].astype(BF)

    def send_b(o):
        px[1, o, 2] = dot(tok_cols(1, shard_of(o, 1)), hid[...], 0, 0).astype(BF)
        net.send(("cb", o), px.at[1, o, 2], sb.at[o, 2], sib)

    def own_b(o):
        px[0, o, 2] = dot(tok_cols(1, shard_of(o, 0)), hid[...], 0, 0).astype(BF)

    def add(dst, *srcs):
        total = dst[...].astype(F32)
        for src in srcs:
            total += src[...].astype(F32)
        dst[...] = total.astype(BF)

    def core_a(o, j):
        net.recv(("ca", o, j), sb.at[o, j], sib)
        add(px.at[0, o, j], sb.at[o, j])

    def core_b(o):
        net.recv(("cb", o), sb.at[o, 2], sib)
        add(px.at[0, o, 2], sb.at[o, 2])

    def far_a(s, d, j):
        net.send(("xh", d, s, j), px.at[0, s, j, pl.ds(d * half, half), :], xh.at[d, s, j], x_to[d])

    def near_a(s, d, j):
        o = 2 + 2 * s + d
        net.recv(("xh", d, s, j), xh.at[d, s, j], x_to[1 - d])
        add(px.at[0, o, j, pl.ds(d * half, half), :], xh.at[d, s, j])
        net.send(("xf", d, s, j), px.at[0, o, j], xf.at[d, s, j], x_to[d])

    def last_a(s, j):
        for d in range(2):
            net.recv(("xf", d, s, j), xf.at[d, s, j], x_to[1 - d])

    def cross_a(j):
        last_a(0, j)
        add(px.at[0, 6, j], xf.at[0, 0, j], xf.at[1, 0, j])
        net.send(("yr", j), px.at[0, 6, j], yr.at[j], far_y)

    B_OTHER, B_OWN = (0, 2, 3, 6), (1, 4, 5, 7)

    def cross_b(i):
        net.send(("by", i), px.at[0, B_OTHER[i], 2], by.at[i], far_y)

    def crossed_b(i):
        net.recv(("by", i), by.at[i], far_y)
        add(px.at[0, B_OWN[i], 2], by.at[i])

    def far_b(d):
        net.send(("bh", d), px.at[0, 1, 2, pl.ds(d * half, half), :], bh.at[d], x_to[d])

    def near_b(d):
        o = B_OWN[1 + d]
        net.recv(("bh", d), bh.at[d], x_to[1 - d])
        add(px.at[0, o, 2, pl.ds(d * half, half), :], bh.at[d])
        net.send(("bf", d), px.at[0, o, 2], bf.at[d], x_to[d])

    def token_part(q, h):
        @pl.loop(2 * h, 2 * h + 2)
        def _(i):
            d = q * (dm // dd // Q) + i
            part = dot(gc[:, :ff], w[d, 0], 1, 1) + dot(gc[:, ff:], w[d, 1], 1, 1)
            part = part.reshape(16, rows, dd).astype(BF)
            for n, (l, steps) in enumerate(ARRIVAL):
                gt[q, steps, l, :, columns(i)] = part[n]

    def gt_ref(q, steps):
        return gt.at[q, steps % NZ]

    def z_far(q):
        d = q // 2
        net.send(("z1", d, q % 2), gt_ref(q, 4), z1.at[d, q % 2], z_to[d])

    def z_near(k, q, d):
        ref = gt_ref(q, sign[d] * (3 - k))
        if k > 0:
            net.recv(("zr", d, k - 1, q), zr.at[d, k - 1, q], z_to[1 - d])
            add(ref, zr.at[d, k - 1, q])
        elif q // 2 == d:
            net.recv(("z1", d, q % 2), z1.at[d, q % 2], z_to[1 - d])
            add(ref, z1.at[d, q % 2])
        net.send(("zr", d, k, q), ref, zr.at[d, k, q], z_to[d])

    def z_last(q):
        for d in range(2):
            net.recv(("zr", d, 2, q), zr.at[d, 2, q], z_to[1 - d])
        add(gt.at[q, 0, 1], zr.at[0, 2, q, 1], zr.at[1, 2, q, 1])
        net.send(("lr", q), gt.at[q, 0, 1], lr.at[q], near_y)

    done = []

    def write(src, dst):
        copy = pltpu.make_async_copy(src, dst, out_sem.at[len(done)])
        copy.start()
        done.append(copy)

    def l_last(q):
        net.recv(("lr", q), lr.at[q], near_y)
        part = pl.ds(q * qc, qc)
        s_tok[:, part] = (
            gt[q, 0, 0].astype(F32) + zr[0, 2, q, 0].astype(F32)
            + zr[1, 2, q, 0].astype(F32) + lr[q].astype(F32)
        ).astype(BF)
        write(s_tok.at[:, part], o_tok.at[:, part])

    def end_a(j):
        last_a(1, j)
        net.recv(("yr", j), yr.at[j], far_y)
        s_w[j] = (
            px[0, 7, j].astype(F32) + xf[0, 1, j].astype(F32)
            + xf[1, 1, j].astype(F32) + yr[j].astype(F32)
        ).astype(BF)
        write(s_w.at[j], (o_gate, o_up)[j])

    def end_b():
        for d in range(2):
            net.recv(("bf", d), bf.at[d], x_to[1 - d])
        dws[...] = (
            px[0, 7, 2].astype(F32) + bf[0].astype(F32) + bf[1].astype(F32)
        ).T.astype(BF)
        write(dws, o_down)

    grad_h()
    send_a(0)
    token_part(0, 1)
    token_part(0, 0)
    z_near(0, 0, 1)
    z_far(0)
    own_a(0)
    core_a(0, 1)
    far_a(0, 0, 1)
    far_a(0, 1, 1)
    send_b(2)
    token_part(2, 1)
    token_part(2, 0)
    z_far(2)
    z_near(0, 2, 0)
    core_a(0, 0)
    far_a(0, 0, 0)
    own_b(2)
    core_b(2)
    cross_b(1)
    far_a(0, 1, 0)
    send_a(1)
    token_part(1, 0)
    send_b(0)
    z_near(1, 0, 1)
    z_near(0, 0, 0)
    own_a(1)
    core_a(1, 1)
    far_a(1, 0, 1)
    far_a(1, 1, 1)
    token_part(1, 1)
    own_b(0)
    core_b(0)
    z_near(0, 1, 1)
    core_a(1, 0)
    far_a(1, 1, 0)
    far_a(1, 0, 0)
    z_far(1)
    send_a(2)
    cross_b(0)
    z_near(1, 2, 0)
    send_a(3)
    own_a(2)
    send_b(6)
    z_near(0, 2, 1)
    own_a(3)
    core_a(2, 0)
    near_a(0, 0, 0)
    core_a(3, 0)
    near_a(0, 1, 0)
    token_part(3, 0)
    token_part(3, 1)
    z_far(3)
    z_near(1, 0, 0)
    core_a(3, 1)
    own_b(6)
    near_a(0, 1, 1)
    core_b(6)
    cross_b(3)
    core_a(2, 1)
    send_a(5)
    near_a(0, 0, 1)
    z_near(2, 0, 1)
    z_near(0, 1, 0)
    own_a(5)
    own_b(4)
    send_b(1)
    z_near(1, 2, 1)
    send_b(3)
    own_a(6)
    send_a(4)
    own_b(3)
    send_a(6)
    z_near(0, 3, 0)
    own_b(7)
    z_near(0, 3, 1)
    z_near(1, 1, 1)
    core_b(3)
    cross_b(2)
    own_b(1)
    core_b(1)
    crossed_b(0)
    own_a(4)
    far_b(1)
    send_a(7)
    z_near(2, 0, 0)
    far_b(0)
    send_b(5)
    core_a(6, 1)
    core_a(4, 0)
    core_a(5, 0)
    near_a(1, 1, 0)
    core_a(6, 0)
    cross_a(0)
    near_a(1, 0, 0)
    own_b(5)
    send_b(4)
    z_near(1, 1, 0)
    core_a(5, 1)
    own_a(7)
    z_near(1, 3, 0)
    core_b(4)
    crossed_b(1)
    z_near(2, 2, 1)
    z_last(0)
    z_near(2, 2, 0)
    core_b(5)
    crossed_b(2)
    near_b(1)
    send_b(7)
    near_b(0)
    z_near(1, 3, 1)
    cross_a(1)
    core_a(4, 1)
    z_near(2, 1, 1)
    core_a(7, 1)
    core_a(7, 0)
    near_a(1, 1, 1)
    z_near(2, 1, 0)
    z_near(2, 3, 0)
    near_a(1, 0, 1)
    z_near(2, 3, 1)
    core_b(7)
    crossed_b(3)
    z_last(2)
    end_a(0)
    z_last(1)
    end_b()
    z_last(3)
    l_last(2)
    l_last(0)
    l_last(1)
    end_a(1)
    l_last(3)
    for copy in done:
        copy.wait()
    net.finish()
    assert len(net.index) <= N_COPIES


def deliver(a, b, c, d, to_a, to_b, to_c, to_d, at_a, at_b, at_c, at_d, in_sem, out_sem):
    taken = [
        pltpu.make_async_copy(src, at, in_sem.at[i])
        for i, (src, at) in enumerate(((a, at_a), (b, at_b), (c, at_c), (d, at_d)))
    ]
    given = [
        pltpu.make_async_copy(at, dst, out_sem.at[i])
        for i, (at, dst) in enumerate(((at_a, to_a), (at_b, to_b), (at_c, to_c), (at_d, to_d)))
    ]
    for copy in taken:
        copy.start()
    for copy_in, copy_out in zip(taken, given):
        copy_in.wait()
        copy_out.start()
    for copy in given:
        copy.wait()


def local(tokens, grad_out, gate_weight, up_weight, down_weight):
    rows, dm = tokens.shape
    dd, ff = gate_weight.shape
    qc = dm // Q
    any_space = pl.BlockSpec(memory_space=pl.ANY)
    out = pl.pallas_call(
        kernel,
        out_shape=(
            jax.ShapeDtypeStruct((rows, dm), BF),
            jax.ShapeDtypeStruct((dd, ff), BF),
            jax.ShapeDtypeStruct((dd, ff), BF),
            jax.ShapeDtypeStruct((ff, dd), BF),
        ),
        in_specs=[any_space] * 5,
        out_specs=[any_space] * 4,
        scratch_shapes=[
            pltpu.VMEM((16, 2, rows, dm), BF),
            pltpu.VMEM((16, 3, dd, ff), BF),
            pltpu.VMEM((3, 16 * rows, ff), F32),
            pltpu.VMEM((16 * rows, 2 * ff), BF),
            pltpu.VMEM((16 * rows, ff), BF),
            pltpu.VMEM((2, 8, 3, dd, ff), BF),
            pltpu.VMEM((8, 3, dd, ff), BF),
            pltpu.VMEM((2, 2, 2, dd // 2, ff), BF),
            pltpu.VMEM((2, 2, 2, dd, ff), BF),
            pltpu.VMEM((2, dd, ff), BF),
            pltpu.VMEM((2, dd // 2, ff), BF),
            pltpu.VMEM((2, dd, ff), BF),
            pltpu.VMEM((4, dd, ff), BF),
            pltpu.VMEM((Q, NZ, 2, rows, qc), BF),
            pltpu.VMEM((2, 2, 2, rows, qc), BF),
            pltpu.VMEM((2, 3, Q, 2, rows, qc), BF),
            pltpu.VMEM((Q, rows, qc), BF),
            pltpu.VMEM((ff, dd), BF),
            pltpu.VMEM((rows, dm), BF),
            pltpu.VMEM((2, dd, ff), BF),
            pltpu.SemaphoreType.DMA((N_COPIES,)),
            pltpu.SemaphoreType.DMA((N_COPIES,)),
            pltpu.SemaphoreType.DMA((5,)),
            pltpu.SemaphoreType.DMA((7,)),
        ],
        compiler_params=pltpu.CompilerParams(
            collective_id=0, has_side_effects=True, vmem_limit_bytes=63 * 1024 * 1024
        ),
    )(tokens, grad_out, gate_weight, up_weight, down_weight)
    return pl.pallas_call(
        deliver,
        out_shape=tuple(jax.ShapeDtypeStruct(a.shape, BF) for a in out),
        in_specs=[any_space] * 4,
        out_specs=[any_space] * 4,
        scratch_shapes=[
            *(pltpu.VMEM(a.shape, BF) for a in out),
            pltpu.SemaphoreType.DMA((4,)),
            pltpu.SemaphoreType.DMA((4,)),
        ],
        compiler_params=pltpu.CompilerParams(vmem_limit_bytes=63 * 1024 * 1024),
    )(*out)


def solution(mesh):
    return jax.shard_map(
        local,
        mesh=mesh,
        in_specs=(
            P(("dp", "tensor"), None),
            P(("dp", "tensor"), None),
            P("dp", "tensor"),
            P("dp", "tensor"),
            P("tensor", "dp"),
        ),
        out_specs=(
            P(("dp", "tensor"), None),
            P("dp", "tensor"),
            P("dp", "tensor"),
            P("tensor", "dp"),
        ),
        check_vma=False,
    )
```
